128 devices in a mesh: lon: 16 (over x, z_hi, core), lat: 8 (over z_lo, y).
Axes of the slice: x: 4, y: 4, z: 4 (z_hi: 2, z_lo: 2; z = z_hi * 2 + z_lo), core: 2. Of those that a mesh axis runs over, the one named last changes fastest.
Arguments:
- features: bfloat16 [128, 2048, 256], P('lat', 'lon'), may hold values from -6 to 6
- cotangent: bfloat16 [128, 2048, 256], P('lat', 'lon'), may hold values from -6 to 6
- land_sea: int32 [128, 2048], P('lat', 'lon'), may hold values from 0 to 1, as said below
- tile_slot: int32 [128, 16], P('lat', 'lon'), may hold values from 0 to 64, as said below
- kernel: float32 [7, 7, 256], replicated, may hold values from -0.875 to 0.875
- ln_gain: float32 [256], replicated, may hold values from 0.5 to 1.5
- ln_bias: float32 [256], replicated, may hold values from -3 to 3
- w_in: bfloat16 [256, 1024], replicated, may hold values from -0.375 to 0.375
- b_in: float32 [1024], replicated, may hold values from -3 to 3
- w_out: bfloat16 [1024, 256], replicated, may hold values from -0.1875 to 0.1875
- layer_scale: float32 [256], replicated, may hold values from 0.3 to 1.5
Outputs:
- output: bfloat16 [128, 2048, 256], P('lat', 'lon')
- grad_features: bfloat16 [128, 2048, 256], P('lat', 'lon')
- grad_w_in: float32 [256, 1024], replicated
- grad_w_out: float32 [1024, 256], replicated
- grad_kernel: float32 [7, 7, 256], replicated
- grad_layer_scale: float32 [256], replicated
The draws below stay inside these ranges and needn't reach their ends.
Inputs may be any that keep to these rules, and one draw needn't show every extreme that they name: `tile_slot`: in each longitude column a value v < 64 names an owner band v // 8 and a slot v % 8 there, distinct within the column; 64 marks a tile without work. Of one device's tiles at most 2 name any one other band, a bound reached in every draw; some owner has all 8 slots taken in every column. `land_sea`: every cell of a tile whose tile_slot is 64 is land.
All inputs are finite; a program needn't handle non-finite values.
Results may differ from the reference program's by a relative error of at most 0.012.
Values may be sent and summed in bfloat16 or wider, within the bound.
No kernel may reach another device: no remote copies, remote signals or barrier semaphores. Data moves between devices by JAX's collectives and lax.ppermute only.
A program may use at most 64 MiB of HBM per device.

```python
import math
import jax
import jax.numpy as jnp
from jax import lax

C = 256
FF = 1024
KS = 7
TILE = 128
SEND = 2
ROWS = 16
CAP = 8
SLOTS = 64
NLAT = 128
NLON = 2048


def column_owners(key):
    band_count = NLAT // ROWS
    half_bands = band_count // 2
    key_order, key_flow, key_room, key_rows = jax.random.split(key, 4)
    shuffle = jax.random.permutation(key_order, band_count)
    senders = shuffle[:half_bands]
    takers = shuffle[half_bands:]
    flow_counts = jax.random.randint(key_flow, (half_bands, half_bands), 0, SEND + 1).at[0, 0].set(SEND)
    sent_total = jnp.sum(flow_counts, axis=1)
    taken_total = jnp.sum(flow_counts, axis=0)
    spare_room = jax.random.randint(key_room, (half_bands,), 0, CAP - SEND * half_bands + 1).at[0].set(0)
    wet_count = jnp.zeros((band_count,), jnp.int32).at[senders].set(CAP + sent_total).at[takers].set(CAP - taken_total - spare_room)
    scores = jax.random.randint(key_rows, (band_count, ROWS), 0, 1 << 20) * ROWS + jnp.arange(ROWS, dtype=jnp.int32)[None, :]
    row_order = jnp.argsort(jnp.argsort(scores, axis=1), axis=1)
    is_wet = row_order < wet_count[:, None]
    wet_rank = jnp.cumsum(is_wet.astype(jnp.int32), axis=1) - 1
    position = jnp.argsort(shuffle)
    sender_pos = jnp.minimum(position, half_bands - 1)
    flow_ends = jnp.cumsum(flow_counts, axis=1)[sender_pos]
    extra_rank = wet_rank - CAP
    receiver_pos = jnp.sum((flow_ends[:, None, :] <= extra_rank[:, :, None]).astype(jnp.int32), axis=2)
    receiver_pos = jnp.minimum(receiver_pos, half_bands - 1)
    flow_start = jnp.take_along_axis(flow_ends - flow_counts[sender_pos], receiver_pos, axis=1)
    before = jnp.cumsum(flow_counts, axis=0) - flow_counts
    receiver = takers[receiver_pos]
    offset = before[sender_pos[:, None], receiver_pos]
    moved_slot = receiver * CAP + wet_count[receiver] + offset + (extra_rank - flow_start)
    band_ids = jnp.arange(band_count, dtype=jnp.int32)[:, None]
    tile_value = jnp.where(wet_rank < CAP, band_ids * CAP + wet_rank, moved_slot)
    return jnp.where(is_wet, tile_value, SLOTS).astype(jnp.int32)


def owner_table(key):
    columns = NLON // TILE
    column_keys = jax.random.split(key, columns)
    tables = jax.vmap(column_owners)(column_keys)
    return tables.reshape(columns, NLAT).T


def draw_tile_slot(key, part):
    return owner_table(key)


def draw_land_sea(key, part):
    table = owner_table(key)
    key = jax.random.fold_in(key, 11)
    columns = NLON // TILE
    coins = jax.random.randint(key, (NLAT, columns, TILE), 0, 20) < 17
    cells = (table < SLOTS)[:, :, None] & coins
    return cells.reshape(NLAT, NLON).astype(jnp.int32)


def level_of(own_key, dims, pieces, smallest, largest):
    def one(axis_at, blocks):
        steps = jax.random.uniform(jax.random.fold_in(jax.random.fold_in(own_key, 6), axis_at), (blocks,), jnp.float32, smallest / len(pieces), largest / len(pieces))
        return jnp.repeat(jnp.exp(steps), dims[axis_at] // blocks).reshape((-1,) + (1,) * (len(dims) - axis_at - 1))

    gain = one(*pieces[0])
    for cut in pieces[1:]:
        gain = gain * one(*cut)
    return gain


def gaussian(rng, extent, spread, limit, shards=(), held_as=jnp.bfloat16):
    values = spread * jax.random.normal(rng, extent, jnp.float32)
    if shards:
        values = values * level_of(rng, extent, shards, -0.22, 0.18)
    return jnp.clip(values, -limit, limit).astype(held_as)


def setup_inputs(seed: int = 0) -> dict:
    key_list = jax.random.split(jax.random.key(seed), 12)
    features = gaussian(key_list[0], (NLAT, NLON, C), 1.0, 6.0, ((0, 8), (1, 16)))
    cotangent = gaussian(key_list[1], (NLAT, NLON, C), 1.0, 6.0, ((0, 8), (1, 16)))
    land_sea = draw_land_sea(jax.random.fold_in(key_list[11], 71), 0)
    tile_slot = draw_tile_slot(jax.random.fold_in(key_list[11], 71), 0)
    kernel = gaussian(key_list[4], (KS, KS, C), (KS * KS) ** -0.5, 0.875, (), jnp.float32)
    ln_gain = jnp.clip(1.0 + 0.1 * jax.random.normal(key_list[5], (C,), jnp.float32), 0.5, 1.5)
    ln_bias = gaussian(key_list[6], (C,), 0.3, 3.0, (), jnp.float32)
    w_in = gaussian(key_list[7], (C, FF), C ** -0.5, 0.375)
    b_in = gaussian(key_list[8], (FF,), 0.5, 3.0, (), jnp.float32)
    w_out = gaussian(key_list[9], (FF, C), FF ** -0.5, 0.1875)
    layer_scale = jnp.clip(jnp.exp(jax.random.uniform(key_list[10], (C,), jnp.float32, math.log(0.3), math.log(1.5))), 0.3, 1.5)
    return {"features": features, "cotangent": cotangent, "land_sea": land_sea, "tile_slot": tile_slot, "kernel": kernel, "ln_gain": ln_gain, "ln_bias": ln_bias, "w_in": w_in, "b_in": b_in, "w_out": w_out, "layer_scale": layer_scale}


GELU_SCALE = math.sqrt(2.0 / math.pi)
GELU_CUBE = 0.044715
EPSILON = 1e-06

def gelu_parts(hidden):
    inside = GELU_SCALE * (hidden + GELU_CUBE * hidden * hidden * hidden)
    hyper = jnp.tanh(inside)
    activated = 0.5 * hidden * (1.0 + hyper)
    derivative = 0.5 * (1.0 + hyper) + 0.5 * hidden * (1.0 - hyper * hyper) * GELU_SCALE * (1.0 + 3.0 * GELU_CUBE * hidden * hidden)
    return (activated, derivative)

def extend_rim(field):
    margin = KS // 2
    wrapped = jnp.concatenate([field[:, -margin:], field, field[:, :margin]], axis=1)
    return jnp.pad(wrapped, ((margin, margin), (0, 0), (0, 0)))

def pointwise(norm_rows, grad_rows, w_in, b_in, w_out):
    hidden = jnp.dot(norm_rows, w_in, preferred_element_type=jnp.float32) + b_in
    activated, derivative = gelu_parts(hidden)
    act_low = activated.astype(jnp.bfloat16)
    result = jnp.dot(act_low, w_out, preferred_element_type=jnp.float32).astype(jnp.bfloat16)
    grad_act = jnp.dot(grad_rows, w_out.T, preferred_element_type=jnp.float32)
    grad_hidden = (grad_act * derivative).astype(jnp.bfloat16)
    grad_wo = jnp.dot(act_low.T, grad_rows, preferred_element_type=jnp.float32)
    grad_wi = jnp.dot(norm_rows.T, grad_hidden, preferred_element_type=jnp.float32)
    grad_norm = jnp.dot(grad_hidden, w_in.T, preferred_element_type=jnp.float32).astype(jnp.bfloat16)
    return (result, grad_norm, grad_wi, grad_wo)

def reference(features, cotangent, land_sea, tile_slot, kernel, ln_gain, ln_bias, w_in, b_in, w_out, layer_scale):
    padded = extend_rim(features).astype(jnp.float32)
    mixed = jnp.zeros(features.shape, jnp.float32)
    for row_off in range(KS):
        for col_off in range(KS):
            mixed = mixed + kernel[row_off, col_off] * padded[row_off:row_off + NLAT, col_off:col_off + NLON]
    row_mean = lax.optimization_barrier(jnp.mean(mixed, axis=-1, keepdims=True))
    centered = mixed - row_mean
    row_var = lax.optimization_barrier(jnp.mean(centered * centered, axis=-1, keepdims=True))
    inverse_scale = lax.rsqrt(row_var + EPSILON)
    normed = centered * inverse_scale
    normalized = (normed * ln_gain + ln_bias).astype(jnp.bfloat16)
    listed = jnp.repeat((tile_slot < SLOTS).astype(jnp.float32), TILE, axis=1)
    weight_mask = listed * land_sea.astype(jnp.float32)
    branch_gate = weight_mask[:, :, None] * layer_scale
    cot_wide = cotangent.astype(jnp.float32)
    grad_out = (branch_gate * cot_wide).astype(jnp.bfloat16)
    blocks = NLAT * NLON // (ROWS * TILE)
    norm_blocks = normalized.reshape(blocks, ROWS * TILE, C)
    grad_blocks = grad_out.reshape(blocks, ROWS * TILE, C)

    def block_step(carry, pair):
        result, grad_norm, grad_wi, grad_wo = pointwise(pair[0], pair[1], w_in, b_in, w_out)
        return ((carry[0] + grad_wi, carry[1] + grad_wo), (result, grad_norm))
    start = (jnp.zeros((C, FF), jnp.float32), jnp.zeros((FF, C), jnp.float32))
    (sum_w_in, sum_w_out), (results, grad_norms) = lax.scan(block_step, start, (norm_blocks, grad_blocks))
    branch = results.reshape(NLAT, NLON, C).astype(jnp.float32)
    output = (features.astype(jnp.float32) + branch_gate * branch).astype(jnp.bfloat16)
    scale_sum = lax.optimization_barrier(jnp.sum(weight_mask[:, :, None] * cot_wide * branch, axis=(0, 1)))
    grad_normed = grad_norms.reshape(NLAT, NLON, C).astype(jnp.float32) * ln_gain
    grad_mixed = (inverse_scale * (grad_normed - lax.optimization_barrier(jnp.mean(grad_normed, axis=-1, keepdims=True)) - normed * lax.optimization_barrier(jnp.mean(grad_normed * normed, axis=-1, keepdims=True)))).astype(jnp.bfloat16)
    grad_pad = extend_rim(grad_mixed).astype(jnp.float32)
    grad_wide = grad_mixed.astype(jnp.float32)
    grad_features = cot_wide
    kernel_rows = []
    for row_off in range(KS):
        for col_off in range(KS):
            flip_row = KS - 1 - row_off
            flip_col = KS - 1 - col_off
            grad_features = grad_features + kernel[row_off, col_off] * grad_pad[flip_row:flip_row + NLAT, flip_col:flip_col + NLON]
            kernel_rows.append(lax.optimization_barrier(jnp.sum(grad_wide * padded[row_off:row_off + NLAT, col_off:col_off + NLON], axis=(0, 1))))
    factor = 1.0 / math.sqrt(NLAT * NLON)
    grad_kernel = jnp.stack(kernel_rows).reshape(KS, KS, C) * factor
    return (output, grad_features.astype(jnp.bfloat16), sum_w_in * factor, sum_w_out * factor, grad_kernel, scale_sum * factor)
```

```python
import math

import jax
import jax.numpy as jnp
from jax import lax
from jax.experimental import pallas as pl
from jax.experimental.pallas import tpu as pltpu
from jax.sharding import Mesh
from jax.sharding import PartitionSpec as P

KS = 7
MARGIN = KS // 2
HALF = 128
STEP = 8
SPAN = 16
EDGE = 8
TAPS = (KS + 1) // 2 * KS
GELU_SCALE = math.sqrt(2.0 / math.pi)
GELU_CUBE = 0.044715
EPSILON = 1e-06
LON = ("x", "zh", "core")
LAT = ("zl", "y")
CHIPS = ("x", "zh", "zl", "y")
ALL = ("x", "zh", "core", "zl", "y")
F32 = jnp.float32
BF16 = jnp.bfloat16


def dot(a, b):
    return jnp.dot(a, b, preferred_element_type=F32)


def dot_cells(a, b):
    return lax.dot_general(a, b, (((0,), (0,)), ((), ())), preferred_element_type=F32)


def build_weights(taps_ref, w_ref, flip):
    rows = lax.broadcasted_iota(jnp.int32, (HALF, HALF), 0)
    cols = lax.broadcasted_iota(jnp.int32, (HALF, HALF), 1)
    eye = rows == cols
    zero = jnp.zeros((HALF, HALF), F32)
    for h in range(2):
        for i2 in range((KS + 1) // 2):
            for j in range(KS):
                tile = i2 * KS + j
                for a in range(2):
                    for b in range(2):
                        i = 2 * i2 + a - b
                        if 0 <= i < KS:
                            tap = (KS - 1 - i) * KS + (KS - 1 - j) if flip else i * KS + j
                            row = taps_ref[tap : tap + 1, h * HALF : (h + 1) * HALF]
                            block = jnp.where(eye, row, zero)
                        else:
                            block = zero
                        w_ref[
                            h,
                            tile * 256 + a * HALF : tile * 256 + (a + 1) * HALF,
                            b * HALF : (b + 1) * HALF,
                        ] = block.astype(BF16)


def assemble(flag_ref, main_ref, west_ref, east_ref, south_ref, north_ref, wide, xs, xs_wide):
    rows, tile, _ = main_ref.shape
    for h in range(2):
        lanes = slice(h * HALF, (h + 1) * HALF)
        wide[h, 0:MARGIN] = south_ref[:, :, lanes].astype(F32) * flag_ref[0, 0]
        wide[h, rows + MARGIN : rows + 2 * MARGIN] = (
            north_ref[:, :, lanes].astype(F32) * flag_ref[0, 1]
        )

        def place(r, _):
            wide[h, r + MARGIN, EDGE : EDGE + tile, :] = main_ref[r, :, lanes].astype(F32)
            wide[h, r + MARGIN, 0:EDGE, :] = west_ref[r, :, lanes].astype(F32)
            wide[h, r + MARGIN, EDGE + tile : 2 * EDGE + tile, :] = east_ref[r, :, lanes].astype(
                F32
            )
            return 0

        lax.fori_loop(0, rows, place, 0)

        def spread(r, _):
            for t in range(STEP + 2 * MARGIN):
                piece = wide[h, r, pl.ds(EDGE - MARGIN + t, SPAN, stride=STEP), :]
                if xs_wide is not None:
                    xs_wide[h, r, t] = piece
                xs[h, r, t] = piece.astype(BF16)
            return 0

        lax.fori_loop(0, rows + 2 * MARGIN, spread, 0)


def conv_pair(xs, w_ref, h, pair):
    pieces = []
    for i2 in range((KS + 1) // 2):
        for j in range(KS):
            for a in range(2):
                pieces.append(
                    xs[h, 2 * pair + 2 * i2 + a, j : j + STEP].reshape(STEP * SPAN, HALF)
                )
    return dot(jnp.concatenate(pieces, axis=1), w_ref[h])


def forward_kernel(
    flag_ref,
    main_ref,
    west_ref,
    east_ref,
    south_ref,
    north_ref,
    cot_ref,
    mask_ref,
    taps_ref,
    gain_ref,
    bias_ref,
    w_in_ref,
    w_in_t_ref,
    b_in_ref,
    w_out_ref,
    w_out_t_ref,
    scale_ref,
    out_ref,
    gm_ref,
    sums_ref,
    wide,
    xs,
    xs_wide,
    w_ref,
    out_wide,
    gm_wide,
    gm_xs,
    acc_in,
    acc_out,
    acc_scale,
):
    rows = main_ref.shape[0]
    ff = w_in_ref.shape[1]
    width = 2 * HALF
    cells = 2 * STEP * SPAN
    build_weights(taps_ref, w_ref, False)
    assemble(flag_ref, main_ref, west_ref, east_ref, south_ref, north_ref, wide, xs, xs_wide)
    acc_in[...] = jnp.zeros_like(acc_in)
    acc_out[...] = jnp.zeros_like(acc_out)
    acc_scale[...] = jnp.zeros_like(acc_scale)
    gain, bias, scale = gain_ref[...], bias_ref[...], scale_ref[...]

    def pair_step(pair, _):
        low = conv_pair(xs, w_ref, 0, pair)
        high = conv_pair(xs, w_ref, 1, pair)
        mixed = jnp.concatenate(
            [
                jnp.concatenate([low[:, :HALF], high[:, :HALF]], axis=1),
                jnp.concatenate([low[:, HALF:], high[:, HALF:]], axis=1),
            ],
            axis=0,
        )
        mean = jnp.mean(mixed, axis=1, keepdims=True)
        centered = mixed - mean
        var = jnp.mean(centered * centered, axis=1, keepdims=True)
        inverse = lax.rsqrt(var + EPSILON)
        normed = centered * inverse
        normalized = (normed * gain + bias).astype(BF16)
        cot = cot_ref[pl.ds(2 * pair, 2)].reshape(cells, width).astype(F32)
        grad_out = (cot * scale).astype(BF16)
        branch = jnp.zeros((cells, width), F32)
        grad_norm = jnp.zeros((cells, width), F32)
        for f in range(ff // 256):
            part = slice(f * 256, (f + 1) * 256)
            hidden = dot(normalized, w_in_ref[:, part]) + b_in_ref[:, part]
            square = hidden * hidden
            hyper = jnp.tanh(hidden * (GELU_SCALE + GELU_SCALE * GELU_CUBE * square))
            gate = 0.5 + 0.5 * hyper
            act = hidden * gate
            slope = gate + act * (1.0 - gate) * (
                2.0 * GELU_SCALE + 6.0 * GELU_SCALE * GELU_CUBE * square
            )
            act_low = act.astype(BF16)
            grad_hidden = (dot(grad_out, w_out_t_ref[:, part]) * slope).astype(BF16)
            branch = branch + dot(act_low, w_out_ref[part, :])
            grad_norm = grad_norm + dot(grad_hidden, w_in_t_ref[part, :])
            acc_in[:, part] += dot_cells(normalized, grad_hidden)
            acc_out[:, part] += dot_cells(grad_out, act_low)
        branch = branch.astype(BF16).astype(F32)
        acc_scale[...] += jnp.sum((cot * branch).reshape(cells // 8, 8, width), axis=0)
        g = grad_norm.astype(BF16).astype(F32) * gain
        grad_mixed = inverse * (
            g
            - jnp.mean(g, axis=1, keepdims=True)
            - normed * jnp.mean(g * normed, axis=1, keepdims=True)
        )
        grad_mixed = grad_mixed.astype(BF16).astype(F32)
        mask = mask_ref[pl.ds(2 * pair, 2)].reshape(cells, HALF).astype(F32)
        for h in range(2):
            lanes = slice(h * HALF, (h + 1) * HALF)
            added = mask * scale[:, lanes] * branch[:, lanes]
            for b in range(2):
                row = 2 * pair + b
                for t in range(STEP):
                    start = b * STEP * SPAN + t * SPAN
                    feature = xs_wide[h, row + MARGIN, t + MARGIN]
                    out_wide[h, row, pl.ds(t, SPAN, stride=STEP), :] = (
                        feature + added[start : start + SPAN]
                    )
                    piece = grad_mixed[start : start + SPAN, lanes]
                    gm_wide[h, row, pl.ds(t, SPAN, stride=STEP), :] = piece
                    gm_xs[h, row, t] = piece
        return 0

    lax.fori_loop(0, rows // 2, pair_step, 0)

    def finish(r, _):
        for h in range(2):
            lanes = slice(h * HALF, (h + 1) * HALF)
            out_ref[r, :, lanes] = out_wide[h, r].astype(BF16)
            gm_ref[r, :, lanes] = gm_wide[h, r].astype(BF16)
        return 0

    lax.fori_loop(0, rows, finish, 0)
    half_ff = ff // 2
    groups = width // 8

    def pack(group, _):
        for which, acc in enumerate((acc_in, acc_out)):
            for side in range(2):
                sums_ref[which * 2 * groups + group * 2 + side, :, 0:half_ff] = acc[
                    pl.ds(pl.multiple_of(group * 8, 8), 8), side * half_ff : (side + 1) * half_ff
                ].astype(BF16)
        return 0

    lax.fori_loop(0, groups, pack, 0)
    for spot in range(2 * (KS * KS + 1), sums_ref.shape[0]):
        sums_ref[spot, :, half_ff:] = jnp.zeros((8, HALF), BF16)
    for h in range(2):
        lanes = slice(h * HALF, (h + 1) * HALF)
        sums_ref[2 * KS * KS + h, :, half_ff:] = acc_scale[:, lanes].astype(BF16)

        def tap_step(r, sums):
            sums = list(sums)
            for t in range(STEP):
                for side in range(2):
                    part = slice(side * 8, side * 8 + 8)
                    g = gm_xs[h, r, t, part]
                    for i in range(KS):
                        for j in range(KS):
                            sums[i * KS + j] = sums[i * KS + j] + g * xs_wide[h, r + i, t + j, part]
            return tuple(sums)

        sums = lax.fori_loop(
            0, rows, tap_step, tuple(jnp.zeros((8, HALF), F32) for _ in range(KS * KS))
        )
        for tap in range(KS * KS):
            sums_ref[2 * tap + h, :, half_ff:] = sums[tap].astype(BF16)


def backward_kernel(
    flag_ref,
    main_ref,
    west_ref,
    east_ref,
    south_ref,
    north_ref,
    cot_ref,
    taps_ref,
    out_ref,
    wide,
    xs,
    w_ref,
    out_wide,
):
    rows = main_ref.shape[0]
    build_weights(taps_ref, w_ref, True)
    assemble(flag_ref, main_ref, west_ref, east_ref, south_ref, north_ref, wide, xs, None)

    def pair_step(pair, _):
        for h in range(2):
            lanes = slice(h * HALF, (h + 1) * HALF)
            both = conv_pair(xs, w_ref, h, pair)
            for b in range(2):
                for t in range(STEP):
                    out_wide[h, 2 * pair + b, pl.ds(t, SPAN, stride=STEP), :] = both[
                        t * SPAN : (t + 1) * SPAN, b * HALF : (b + 1) * HALF
                    ]
                row = 2 * pair + b
                out_ref[row, :, lanes] = (
                    cot_ref[row, :, lanes].astype(F32) + out_wide[h, row]
                ).astype(BF16)
        return 0

    lax.fori_loop(0, rows // 2, pair_step, 0)


def rim(field):
    rows, tile, width = field.shape
    gap = jnp.zeros((rows, EDGE - MARGIN, width), BF16)
    count = lax.axis_size(LON)
    forward = [(i, (i + 1) % count) for i in range(count)]
    backward = [(i, (i - 1) % count) for i in range(count)]
    west = lax.ppermute(field[:, tile - MARGIN :], LON, forward)
    east = lax.ppermute(field[:, :MARGIN], LON, backward)
    west = jnp.concatenate([gap, west], axis=1)
    east = jnp.concatenate([east, gap], axis=1)
    full = jnp.concatenate([west, field, east], axis=1)
    count = lax.axis_size(LAT)
    forward = [(i, (i + 1) % count) for i in range(count)]
    backward = [(i, (i - 1) % count) for i in range(count)]
    south = lax.ppermute(full[rows - MARGIN :], LAT, forward)
    north = lax.ppermute(full[:MARGIN], LAT, backward)
    return west, east, south, north


def on_device(
    features, cotangent, land_sea, tile_slot, kernel, ln_gain, ln_bias, w_in, b_in, w_out, layer_scale
):
    rows, tile, width = features.shape
    ff = w_in.shape[1]
    devices = lax.axis_size(ALL)
    slot_total = 64
    band = lax.axis_index(LAT)
    flags = jnp.stack([band > 0, band < lax.axis_size(LAT) - 1]).astype(F32).reshape(1, 2)
    taps = kernel.reshape(KS * KS, width)
    mask = (tile_slot < slot_total) & (land_sea > 0)
    cot_masked = jnp.where(mask[:, :, None], cotangent, jnp.zeros_like(cotangent))
    cot_masked = cot_masked.reshape(rows, SPAN, STEP, width).transpose(0, 2, 1, 3)
    mask_wide = jnp.broadcast_to(
        mask.reshape(rows, SPAN, STEP).transpose(0, 2, 1)[..., None].astype(BF16),
        (rows, STEP, SPAN, HALF),
    )
    padded = rows + 2 * MARGIN
    ext = STEP + 2 * MARGIN
    vmem = pl.BlockSpec(memory_space=pltpu.VMEM)
    smem = pl.BlockSpec(memory_space=pltpu.SMEM)
    params = pltpu.CompilerParams(vmem_limit_bytes=56 * 1024 * 1024)
    wide = pltpu.VMEM((2, padded, tile + 2 * EDGE, HALF), F32)
    xs = pltpu.VMEM((2, padded, ext, SPAN, HALF), BF16)
    weights = pltpu.VMEM((2, TAPS * 256, 256), BF16)
    flat = pltpu.VMEM((2, rows, tile, HALF), F32)
    west, east, south, north = rim(features)
    chunk = ff // 2 + HALF
    output, grad_mixed, sums = pl.pallas_call(
        forward_kernel,
        out_shape=(
            jax.ShapeDtypeStruct(features.shape, BF16),
            jax.ShapeDtypeStruct(features.shape, BF16),
            jax.ShapeDtypeStruct((devices, 8, chunk), BF16),
        ),
        in_specs=[smem] + [vmem] * 16,
        out_specs=(vmem, vmem, vmem),
        scratch_shapes=[
            wide,
            xs,
            pltpu.VMEM((2, padded, ext, SPAN, HALF), F32),
            weights,
            flat,
            flat,
            pltpu.VMEM((2, rows, STEP, SPAN, HALF), F32),
            pltpu.VMEM((width, ff), F32),
            pltpu.VMEM((width, ff), F32),
            pltpu.VMEM((8, width), F32),
        ],
        compiler_params=params,
        cost_estimate=pl.CostEstimate(
            flops=14_000_000_000, bytes_accessed=8_000_000, transcendentals=2_000_000
        ),
        name="forward",
    )(
        flags,
        features,
        west,
        east,
        south,
        north,
        cot_masked,
        mask_wide,
        taps,
        ln_gain.reshape(1, width),
        ln_bias.reshape(1, width),
        w_in,
        w_in.T,
        b_in.reshape(1, ff),
        w_out,
        w_out.T,
        layer_scale.reshape(1, width),
    )
    west, east, south, north = rim(grad_mixed)
    arrived = lax.all_to_all(sums, ALL, split_axis=0, concat_axis=0, tiled=True)
    grad_features = pl.pallas_call(
        backward_kernel,
        out_shape=jax.ShapeDtypeStruct(features.shape, BF16),
        in_specs=[smem] + [vmem] * 7,
        out_specs=vmem,
        scratch_shapes=[wide, xs, weights, flat],
        compiler_params=params,
        cost_estimate=pl.CostEstimate(
            flops=7_000_000_000, bytes_accessed=4_000_000, transcendentals=0
        ),
        name="backward",
    )(flags, grad_mixed, west, east, south, north, cotangent, taps)
    own = jnp.sum(arrived.astype(F32), axis=0).astype(BF16)
    chips = lax.axis_size(CHIPS)
    mine = lax.all_to_all(
        jnp.broadcast_to(own[None], (chips,) + own.shape), CHIPS, split_axis=0, concat_axis=0, tiled=True
    )
    other = lax.ppermute(mine, "core", [(0, 1), (1, 0)])
    first = lax.axis_index("core") == 0
    pair = jnp.stack([jnp.where(first, mine, other), jnp.where(first, other, mine)])
    outer = lax.axis_size(("x", "zh"))
    whole = pair.reshape(2, outer, chips // outer, 8, chunk).transpose(1, 0, 2, 3, 4)
    whole = whole.reshape(devices, 8, chunk)
    factor = 1.0 / math.sqrt(rows * lax.axis_size(LAT) * tile * lax.axis_size(LON))
    main = whole[:, :, : ff // 2].reshape(2, width // 8, 2, 8, ff // 2)
    main = main.transpose(0, 1, 3, 2, 4).reshape(2, width, ff).astype(F32) * factor
    small = jnp.sum(whole[: 2 * (KS * KS + 1), :, ff // 2 :].astype(F32), axis=1) * factor
    small = small.reshape(KS * KS + 1, width)
    return (
        output,
        grad_features,
        main[0],
        main[1].T,
        small[: KS * KS].reshape(KS, KS, width),
        small[KS * KS],
    )


def solution(mesh):
    fine = Mesh(mesh.devices.reshape(4, 2, 2, 2, 4), ("x", "zh", "core", "zl", "y"))
    cells = P(LAT, LON, None)
    return jax.shard_map(
        on_device,
        mesh=fine,
        in_specs=(cells, cells, P(LAT, LON), P(LAT, LON)) + (P(),) * 7,
        out_specs=(cells, cells, P(), P(), P(), P()),
        check_vma=False,
    )
```

```python
import functools
import math

import jax
import jax.numpy as jnp
from jax import lax
from jax.experimental import pallas as pl
from jax.experimental.pallas import tpu as pltpu
from jax.sharding import Mesh
from jax.sharding import PartitionSpec as P

KS = 7
MARGIN = KS // 2
HALF = 128
STEP = 8
SPAN = 16
EDGE = 8
SLOTS = 64
FORWARD_VMEM = 56 * 1024 * 1024
BACKWARD_VMEM = 28 * 1024 * 1024
GROUP = 4
CUTS = ((0, 2), (2, 4), (4, 7))
TAPS = (KS + 1) // 2 * KS
GELU_SCALE = math.sqrt(2.0 / math.pi)
GELU_CUBE = 0.044715
EPSILON = 1e-06
LON = ("x", "zh", "core")
LAT = ("zl", "y")
CHIPS = ("x", "zh", "zl", "y")
ALL = ("x", "zh", "core", "zl", "y")
F32 = jnp.float32
BF16 = jnp.bfloat16


def dot(a, b):
    return jnp.dot(a, b, preferred_element_type=F32)


def build_weights(taps_ref, w_ref, flip):
    rows = lax.broadcasted_iota(jnp.int32, (HALF, HALF), 0)
    cols = lax.broadcasted_iota(jnp.int32, (HALF, HALF), 1)
    eye = rows == cols
    zero = jnp.zeros((HALF, HALF), F32)
    for h in range(2):
        for i2 in range((KS + 1) // 2):
            for j in range(KS):
                tile = i2 * KS + j
                for a in range(2):
                    for b in range(2):
                        i = 2 * i2 + a - b
                        if 0 <= i < KS:
                            tap = (KS - 1 - i) * KS + (KS - 1 - j) if flip else i * KS + j
                            row = taps_ref[tap // KS, tap % KS : tap % KS + 1, h * HALF : (h + 1) * HALF]
                            block = jnp.where(eye, row, zero)
                        else:
                            block = zero
                        w_ref[
                            h,
                            tile * 256 + a * HALF : tile * 256 + (a + 1) * HALF,
                            b * HALF : (b + 1) * HALF,
                        ] = block.astype(BF16)


def assemble(main_ref, near_ref, far_ref, south_ref, north_ref, wide, xs):
    rows, tile, _ = main_ref.shape
    even = lax.axis_index("core") == 0
    band = lax.axis_index(LAT)
    below = jnp.where(band > 0, 1.0, 0.0).astype(F32)
    above = jnp.where(band < lax.axis_size(LAT) - 1, 1.0, 0.0).astype(F32)
    for h in range(2):
        lanes = slice(h * HALF, (h + 1) * HALF)
        wide[h, 0:MARGIN] = south_ref[:, :, lanes].astype(F32) * below
        wide[h, rows + MARGIN : rows + 2 * MARGIN] = north_ref[:, :, lanes].astype(F32) * above

    def place(pair, _):
        for r in (2 * pair, 2 * pair + 1):
            for h in range(2):
                lanes = slice(h * HALF, (h + 1) * HALF)
                wide[h, r + MARGIN, EDGE : EDGE + tile, :] = main_ref[r, :, lanes].astype(F32)
                near = near_ref[r, :, lanes].astype(F32)
                far = far_ref[r, :, lanes].astype(F32)
                wide[h, r + MARGIN, 0:EDGE, :] = jnp.where(even, far, near)
                wide[h, r + MARGIN, EDGE + tile : 2 * EDGE + tile, :] = jnp.where(even, near, far)
        return 0

    lax.fori_loop(0, rows // 2, place, 0)

    def spread(pair, _):
        for r in (2 * pair, 2 * pair + 1):
            for h in range(2):
                for t in range(STEP + 2 * MARGIN):
                    piece = wide[h, r, pl.ds(EDGE - MARGIN + t, SPAN, stride=STEP), :]
                    xs[h, r, t] = piece.astype(BF16)
        return 0

    lax.fori_loop(0, rows // 2 + MARGIN, spread, 0)


def stage_cotangent(cot_ref, sea_ref, slot_ref, slots, cot_wide, mask_wide):
    rows, tile, _ = cot_ref.shape
    open_cells = (sea_ref[...] > 0) & (slot_ref[...] < slots)
    mask = jnp.where(open_cells, 1.0, 0.0).astype(F32)
    mask = jnp.concatenate([mask, jnp.zeros((HALF - rows, tile), F32)], axis=0).T
    for r in range(rows):
        column = jnp.broadcast_to(mask[:, r : r + 1], (tile, HALF))
        mask_wide[r] = column
        for h in range(2):
            cot_wide[h, r] = cot_ref[r, :, h * HALF : (h + 1) * HALF].astype(F32) * column


def conv_part(xs, w_ref, h, pair, i2, first, last):
    pieces = []
    for j in range(first, last):
        for a in range(2):
            pieces.append(xs[h, 2 * pair + 2 * i2 + a, j : j + STEP].reshape(STEP * SPAN, HALF))
    span = slice((i2 * KS + first) * 256, (i2 * KS + last) * 256)
    return dot(jnp.concatenate(pieces, axis=1), w_ref[h, span])


def conv_pair(xs, w_ref, h, pair):
    total = conv_part(xs, w_ref, h, pair, 0, 0, KS)
    for i2 in range(1, (KS + 1) // 2):
        total = total + conv_part(xs, w_ref, h, pair, i2, 0, KS)
    return total


def conv_group(xs, w_ref, h, pair):
    pieces = []
    for i2 in range((KS + 1) // 2):
        for j in range(KS):
            for a in range(2):
                rows = [2 * (pair + n) + 2 * i2 + a for n in range(GROUP)]
                pieces.append(
                    jnp.concatenate(
                        [xs[h, r, j : j + STEP].reshape(STEP * SPAN, HALF) for r in rows], axis=0
                    )
                )
    return dot(jnp.concatenate(pieces, axis=1), w_ref[h])


def tap_part(gm_xs, wide, h, i, b, side, pair, sums):
    source = jnp.maximum(pair, 0)
    part = slice(side * 8, side * 8 + 8)
    grads = [gm_xs[h, 2 * pair + 2 + b, t, part] for t in range(STEP)]
    for spot in range(STEP + KS - 1):
        cell = wide[
            h,
            2 * source + b + i,
            pl.ds(EDGE - MARGIN + spot + side * 8 * STEP, 8, stride=STEP),
            :,
        ]
        for j in range(KS):
            if 0 <= spot - j < STEP:
                sums[j] = sums[j] + grads[spot - j] * cell
    return sums


def add_taps(gm_xs, wide, acc_taps, h, i, pair):
    sums = [acc_taps[h, i * KS + j] for j in range(KS)]
    for b in range(2):
        for side in range(2):
            sums = tap_part(gm_xs, wide, h, i, b, side, pair, sums)
    for j in range(KS):
        acc_taps[h, i * KS + j] = sums[j]


def zipped(*lists):
    spots = [((k + 0.5) / len(items), n, k) for n, items in enumerate(lists) for k in range(len(items))]
    return [lists[n][k] for _, n, k in sorted(spots)]


def strided(ref, row):
    return jnp.concatenate(
        [ref[row, pl.ds(t, SPAN, stride=STEP), :] for t in range(STEP)], axis=0
    )


def pack_sums(targets, acc_in, acc_out, acc_scale, acc_taps):
    half_ff = acc_in.shape[1] // 2
    spots = targets[0].shape[0]

    def pack(quad, _):
        for g in range(4):
            group = 4 * quad + g
            for target, acc in zip(targets, (acc_in, acc_out)):
                for side in range(2):
                    target[group * 2 + side, :, 0:half_ff] = acc[
                        pl.ds(pl.multiple_of(group * 8, 8), 8),
                        side * half_ff : (side + 1) * half_ff,
                    ].astype(BF16)
        return 0

    lax.fori_loop(0, spots // 8, pack, 0)
    for spot in range(2 * spots):
        tap, h = spot // 2, spot % 2
        if tap < KS * KS:
            value = acc_taps[h, tap]
        elif tap == KS * KS:
            value = acc_scale[:, h * HALF : (h + 1) * HALF]
        else:
            value = jnp.zeros((8, HALF), F32)
        targets[spot // spots][spot % spots, :, half_ff:] = value.astype(BF16)


def forward_kernel(
    main_ref,
    near_ref,
    far_ref,
    south_ref,
    north_ref,
    cot_ref,
    sea_ref,
    slot_ref,
    taps_ref,
    gain_ref,
    bias_ref,
    w_in_ref,
    w_in_t_ref,
    b_in_ref,
    w_out_ref,
    w_out_t_ref,
    scale_ref,
    out_ref,
    gm_ref,
    keep_ref,
    send_ref,
    wide,
    xs,
    w_ref,
    out_wide,
    gm_wide,
    gm_xs,
    mask_wide,
    mixed_ref,
    acc_taps,
    acc_in,
    acc_out,
    acc_scale,
):
    rows = main_ref.shape[0]
    ff = w_in_ref.shape[1]
    width = 2 * HALF
    cells = 2 * STEP * SPAN
    build_weights(taps_ref, w_ref, False)
    assemble(main_ref, near_ref, far_ref, south_ref, north_ref, wide, xs)
    stage_cotangent(cot_ref, sea_ref, slot_ref, SLOTS, out_wide, mask_wide)
    acc_in[...] = jnp.zeros_like(acc_in)
    acc_out[...] = jnp.zeros_like(acc_out)
    acc_scale[...] = jnp.zeros_like(acc_scale)
    gain, bias, scale = gain_ref[...], bias_ref[...], scale_ref[...]

    acc_taps[...] = jnp.zeros_like(acc_taps)
    for h in range(2):
        gm_xs[h, 0:2] = jnp.zeros((2, STEP, SPAN, HALF), F32)
        mixed_ref[h] = conv_pair(xs, w_ref, h, 0)

    def finish(pair):
        for row in (2 * pair, 2 * pair + 1):
            for h in range(2):
                lanes = slice(h * HALF, (h + 1) * HALF)
                out_ref[row, :, lanes] = out_wide[h, row].astype(BF16)
                gm_ref[row, :, lanes] = gm_wide[h, row].astype(BF16)

    def pair_step(pair, _):
        finish(jnp.maximum(pair - 1, 0))
        low, high = mixed_ref[0], mixed_ref[1]
        mixed = jnp.concatenate(
            [
                jnp.concatenate([low[:, :HALF], high[:, :HALF]], axis=1),
                jnp.concatenate([low[:, HALF:], high[:, HALF:]], axis=1),
            ],
            axis=0,
        )
        later = jnp.minimum(pair + 1, rows // 2 - 1)
        conv_tasks, tap_tasks = [], []
        for h in range(2):
            begun = {}

            def conv_task(h, i2, first, last, begun):
                part = conv_part(xs, w_ref, h, later, i2, first, last)
                begun[0] = part if 0 not in begun else begun[0] + part
                if i2 == (KS - 1) // 2 and last == KS:
                    mixed_ref[h] = begun[0]

            for i2 in range((KS + 1) // 2):
                for first, last in CUTS:
                    conv_tasks.append(functools.partial(conv_task, h, i2, first, last, begun))
            for i in range(KS):
                tap_tasks.append(
                    functools.partial(add_taps, gm_xs, wide, acc_taps, h, i, pair - 1)
                )
        for work in zipped(conv_tasks, tap_tasks):
            work()
        mean = jnp.mean(mixed, axis=1, keepdims=True)
        centered = mixed - mean
        var = jnp.mean(centered * centered, axis=1, keepdims=True)
        inverse = lax.rsqrt(var + EPSILON)
        normed = centered * inverse
        normalized = (normed * gain + bias).astype(BF16)
        cot = jnp.concatenate(
            [
                jnp.concatenate([strided(out_wide.at[h], 2 * pair + b) for b in range(2)], axis=0)
                for h in range(2)
            ],
            axis=1,
        )
        grad_out = (cot * scale).astype(BF16)
        branch = jnp.zeros((cells, width), F32)
        grad_norm = jnp.zeros((cells, width), F32)
        normalized_t = normalized.T
        grad_out_t = grad_out.T
        parts = ff // 256
        def enter(f):
            part = slice(f * 256, (f + 1) * 256)
            return (
                dot(normalized, w_in_ref[:, part]) + b_in_ref[:, part],
                dot(grad_out, w_out_t_ref[:, part]),
            )

        ahead = enter(0)
        for f in range(parts):
            part = slice(f * 256, (f + 1) * 256)
            hidden, grad_act = ahead
            if f + 1 < parts:
                ahead = enter(f + 1)
            square = hidden * hidden
            hyper = jnp.tanh(hidden * (GELU_SCALE + GELU_SCALE * GELU_CUBE * square))
            gate = 0.5 + 0.5 * hyper
            act = hidden * gate
            slope = gate + act * (1.0 - gate) * (
                2.0 * GELU_SCALE + 6.0 * GELU_SCALE * GELU_CUBE * square
            )
            act_low = act.astype(BF16)
            grad_hidden = (grad_act * slope).astype(BF16)
            branch = branch + dot(act_low, w_out_ref[part, :])
            grad_norm = grad_norm + dot(grad_hidden, w_in_t_ref[part, :])
            acc_in[:, part] += dot(normalized_t, grad_hidden)
            acc_out[:, part] += dot(grad_out_t, act_low)
        branch = branch.astype(BF16).astype(F32)
        acc_scale[...] += jnp.sum((cot * branch).reshape(cells // 8, 8, width), axis=0)
        g = grad_norm.astype(BF16).astype(F32) * gain
        grad_mixed = inverse * (
            g
            - jnp.mean(g, axis=1, keepdims=True)
            - normed * jnp.mean(g * normed, axis=1, keepdims=True)
        )
        grad_mixed = grad_mixed.astype(BF16).astype(F32)
        mask = jnp.concatenate([strided(mask_wide, 2 * pair + b) for b in range(2)], axis=0)
        for h in range(2):
            lanes = slice(h * HALF, (h + 1) * HALF)
            added = mask * scale[:, lanes] * branch[:, lanes]
            for b in range(2):
                row = 2 * pair + b
                for t in range(STEP):
                    start = b * STEP * SPAN + t * SPAN
                    feature = wide[h, row + MARGIN, pl.ds(EDGE + t, SPAN, stride=STEP), :]
                    out_wide[h, row, pl.ds(t, SPAN, stride=STEP), :] = (
                        feature + added[start : start + SPAN]
                    )
                    piece = grad_mixed[start : start + SPAN, lanes]
                    gm_wide[h, row, pl.ds(t, SPAN, stride=STEP), :] = piece
                    gm_xs[h, row + 2, t] = piece
        return 0

    lax.fori_loop(0, rows // 2, pair_step, 0)

    finish(rows // 2 - 1)
    for h in range(2):
        for i in range(KS):
            add_taps(gm_xs, wide, acc_taps, h, i, rows // 2 - 1)
    core = lax.axis_index("core")

    @pl.when(core == 0)
    def _():
        pack_sums((keep_ref, send_ref), acc_in, acc_out, acc_scale, acc_taps)

    @pl.when(core != 0)
    def _():
        pack_sums((send_ref, keep_ref), acc_in, acc_out, acc_scale, acc_taps)


def backward_kernel(
    main_ref,
    near_ref,
    far_ref,
    south_ref,
    north_ref,
    cot_ref,
    taps_ref,
    out_ref,
    wide,
    xs,
    w_ref,
    out_wide,
):
    rows = main_ref.shape[0]
    build_weights(taps_ref, w_ref, True)
    assemble(main_ref, near_ref, far_ref, south_ref, north_ref, wide, xs)

    def finish(group, h):
        lanes = slice(h * HALF, (h + 1) * HALF)
        for b in range(2 * GROUP):
            row = 2 * GROUP * group + b
            out_ref[row, :, lanes] = (
                cot_ref[row, :, lanes].astype(F32) + out_wide[h, row]
            ).astype(BF16)

    def group_step(group, _):
        for h in range(2):
            both = conv_group(xs, w_ref, h, GROUP * group)
            for n in range(GROUP):
                for b in range(2):
                    for t in range(STEP):
                        start = (n * STEP + t) * SPAN
                        row = 2 * (GROUP * group + n) + b
                        out_wide[h, row, pl.ds(t, SPAN, stride=STEP), :] = both[
                            start : start + SPAN, b * HALF : (b + 1) * HALF
                        ]
            finish(group, h)
        return 0

    lax.fori_loop(0, rows // 2 // GROUP, group_step, 0)


def rim_sides(field):
    tile = field.shape[1]
    even = lax.axis_index("core") == 0
    low, high = field[:, :EDGE], field[:, tile - EDGE :]
    count = lax.axis_size(LON)
    across = [(i, (i + 1) % count) for i in range(1, count, 2)]
    across += [(target, source) for source, target in across]
    far = lax.ppermute(jnp.where(even, low, high), LON, across)
    near = lax.ppermute(jnp.where(even, high, low), "core", [(0, 1), (1, 0)])
    return near, far


def rim_messages(field, near, far):
    rows = field.shape[0]
    even = lax.axis_index("core") == 0

    def across(part):
        west = jnp.where(even, far[part], near[part])
        east = jnp.where(even, near[part], far[part])
        return jnp.concatenate([west, field[part], east], axis=1)

    return across(slice(rows - MARGIN, rows)), across(slice(0, MARGIN))


def rim_ends(up, down):
    count = lax.axis_size(LAT)
    forward = [(i, (i + 1) % count) for i in range(count)]
    backward = [(i, (i - 1) % count) for i in range(count)]
    return lax.ppermute(up, LAT, forward), lax.ppermute(down, LAT, backward)


def on_device(
    features, cotangent, land_sea, tile_slot, kernel, ln_gain, ln_bias, w_in, b_in, w_out, layer_scale
):
    rows, tile, width = features.shape
    ff = w_in.shape[1]
    chips = lax.axis_size(CHIPS)
    padded = rows + 2 * MARGIN
    ext = STEP + 2 * MARGIN
    vmem = pl.BlockSpec(memory_space=pltpu.VMEM)
    wide = pltpu.VMEM((2, padded, tile + 2 * EDGE, HALF), F32)
    xs = pltpu.VMEM((2, padded, ext, SPAN, HALF), BF16)
    weights = pltpu.VMEM((2, TAPS * 256, 256), BF16)
    flat = pltpu.VMEM((2, rows, tile, HALF), F32)
    near, far = rim_sides(features)
    south, north = rim_ends(*rim_messages(features, near, far))
    chunk = ff // 2 + HALF
    output, grad_mixed, keep, send = pl.pallas_call(
        forward_kernel,
        out_shape=(
            jax.ShapeDtypeStruct(features.shape, BF16),
            jax.ShapeDtypeStruct(features.shape, BF16),
            jax.ShapeDtypeStruct((chips, 8, chunk), BF16),
            jax.ShapeDtypeStruct((chips, 8, chunk), BF16),
        ),
        in_specs=[vmem] * 17,
        out_specs=(vmem,) * 4,
        scratch_shapes=[
            wide,
            xs,
            weights,
            flat,
            flat,
            pltpu.VMEM((2, rows + 2, STEP, SPAN, HALF), F32),
            pltpu.VMEM((rows, tile, HALF), F32),
            pltpu.VMEM((2, STEP * SPAN, 256), F32),
            pltpu.VMEM((2, KS * KS, 8, HALF), F32),
            pltpu.VMEM((width, ff), F32),
            pltpu.VMEM((width, ff), F32),
            pltpu.VMEM((8, width), F32),
        ],
        compiler_params=pltpu.CompilerParams(vmem_limit_bytes=FORWARD_VMEM),
        cost_estimate=pl.CostEstimate(
            flops=14_000_000_000, bytes_accessed=8_000_000, transcendentals=2_000_000
        ),
        name="forward",
    )(
        features,
        near,
        far,
        south,
        north,
        cotangent,
        land_sea,
        tile_slot,
        kernel,
        ln_gain.reshape(1, width),
        ln_bias.reshape(1, width),
        w_in,
        w_in.T,
        b_in.reshape(1, ff),
        w_out,
        w_out.T,
        layer_scale.reshape(1, width),
    )
    swap = [(0, 1), (1, 0)]
    near, far = rim_sides(grad_mixed)
    sums = (keep.astype(F32) + lax.ppermute(send, "core", swap).astype(F32)).astype(BF16)
    south, north = rim_ends(*rim_messages(grad_mixed, near, far))
    arrived = lax.all_to_all(sums, CHIPS, split_axis=0, concat_axis=0, tiled=True)
    own, grad_mixed, near, far, south, north = lax.optimization_barrier(
        (
            jnp.sum(arrived.astype(F32), axis=0).astype(BF16),
            grad_mixed,
            near,
            far,
            south,
            north,
        )
    )
    mine = lax.all_to_all(
        jnp.broadcast_to(own[None], (chips,) + own.shape), CHIPS, split_axis=0, concat_axis=0, tiled=True
    )
    grad_features = pl.pallas_call(
        backward_kernel,
        out_shape=jax.ShapeDtypeStruct(features.shape, BF16),
        in_specs=[vmem] * 7,
        out_specs=vmem,
        scratch_shapes=[wide, xs, weights, flat],
        compiler_params=pltpu.CompilerParams(vmem_limit_bytes=BACKWARD_VMEM),
        cost_estimate=pl.CostEstimate(
            flops=7_000_000_000, bytes_accessed=4_000_000, transcendentals=0
        ),
        name="backward",
    )(grad_mixed, near, far, south, north, cotangent, kernel)
    mine, grad_features = lax.optimization_barrier((mine, grad_features))
    other = lax.ppermute(mine, "core", swap)
    first = lax.axis_index("core") == 0
    whole = jnp.stack([jnp.where(first, mine, other), jnp.where(first, other, mine)])
    factor = 1.0 / math.sqrt(rows * lax.axis_size(LAT) * tile * lax.axis_size(LON))
    main = whole[..., : ff // 2].reshape(2, width // 8, 2, 8, ff // 2)
    main = main.transpose(0, 1, 3, 2, 4).reshape(2, width, ff).astype(F32) * factor
    small = whole[..., ff // 2 :].reshape(2 * chips, 8, HALF)[: 2 * (KS * KS + 1)]
    small = jnp.sum(small.astype(F32), axis=1) * factor
    small = small.reshape(KS * KS + 1, width)
    return (
        output,
        grad_features,
        main[0],
        main[1].T,
        small[: KS * KS].reshape(KS, KS, width),
        small[KS * KS],
    )


def solution(mesh):
    fine = Mesh(mesh.devices.reshape(4, 2, 2, 2, 4), ("x", "zh", "core", "zl", "y"))
    cells = P(LAT, LON, None)
    return jax.shard_map(
        on_device,
        mesh=fine,
        in_specs=(cells, cells, P(LAT, LON), P(LAT, LON)) + (P(),) * 7,
        out_specs=(cells, cells, P(), P(), P(), P()),
        check_vma=False,
    )
```

```python
import functools
import math

import jax
import jax.numpy as jnp
from jax import lax
from jax.experimental import pallas as pl
from jax.experimental.pallas import tpu as pltpu
from jax.sharding import Mesh
from jax.sharding import PartitionSpec as P

KS = 7
MARGIN = KS // 2
HALF = 128
STEP = 8
SPAN = 16
EDGE = 8
SLOTS = 64
FORWARD_VMEM = 36 * 1024 * 1024
BACKWARD_VMEM = 28 * 1024 * 1024
GROUP = 4
CUTS = ((0, 2), (2, 4), (4, 7))
TAPS = (KS + 1) // 2 * KS
GELU_SCALE = math.sqrt(2.0 / math.pi)
GELU_CUBE = 0.044715
EPSILON = 1e-06
LON = ("x", "zh", "core")
LAT = ("zl", "y")
CHIPS = ("x", "zh", "zl", "y")
ALL = ("x", "zh", "core", "zl", "y")
F32 = jnp.float32
BF16 = jnp.bfloat16


def dot(a, b):
    return jnp.dot(a, b, preferred_element_type=F32)


def dot_flipped(a, b):
    return lax.dot_general(a, b, (((1,), (1,)), ((), ())), preferred_element_type=F32)


def build_weights(taps_ref, w_ref, flip):
    rows = lax.broadcasted_iota(jnp.int32, (HALF, HALF), 0)
    cols = lax.broadcasted_iota(jnp.int32, (HALF, HALF), 1)
    eye = rows == cols
    zero = jnp.zeros((HALF, HALF), F32)
    for h in range(2):
        for i2 in range((KS + 1) // 2):
            for j in range(KS):
                tile = i2 * KS + j
                for a in range(2):
                    for b in range(2):
                        i = 2 * i2 + a - b
                        if 0 <= i < KS:
                            tap = (KS - 1 - i) * KS + (KS - 1 - j) if flip else i * KS + j
                            row = taps_ref[tap // KS, tap % KS : tap % KS + 1, h * HALF : (h + 1) * HALF]
                            block = jnp.where(eye, row, zero)
                        else:
                            block = zero
                        w_ref[
                            h,
                            tile * 256 + a * HALF : tile * 256 + (a + 1) * HALF,
                            b * HALF : (b + 1) * HALF,
                        ] = block.astype(BF16)


def assemble(main_ref, near_ref, far_ref, south_ref, north_ref, wide, xs, xs_wide=None):
    rows, tile, _ = main_ref.shape
    even = lax.axis_index("core") == 0
    band = lax.axis_index(LAT)
    below = jnp.where(band > 0, 1.0, 0.0).astype(F32)
    above = jnp.where(band < lax.axis_size(LAT) - 1, 1.0, 0.0).astype(F32)
    for h in range(2):
        lanes = slice(h * HALF, (h + 1) * HALF)
        wide[h, 0:MARGIN] = south_ref[:, :, lanes].astype(F32) * below
        wide[h, rows + MARGIN : rows + 2 * MARGIN] = north_ref[:, :, lanes].astype(F32) * above

    def place(pair, _):
        for r in (2 * pair, 2 * pair + 1):
            for h in range(2):
                lanes = slice(h * HALF, (h + 1) * HALF)
                wide[h, r + MARGIN, EDGE : EDGE + tile, :] = main_ref[r, :, lanes].astype(F32)
                near = near_ref[r, :, lanes].astype(F32)
                far = far_ref[r, :, lanes].astype(F32)
                wide[h, r + MARGIN, 0:EDGE, :] = jnp.where(even, far, near)
                wide[h, r + MARGIN, EDGE + tile : 2 * EDGE + tile, :] = jnp.where(even, near, far)
        return 0

    lax.fori_loop(0, rows // 2, place, 0)

    def spread(pair, _):
        for r in (2 * pair, 2 * pair + 1):
            for h in range(2):
                for t in range(STEP + 2 * MARGIN):
                    piece = wide[h, r, pl.ds(EDGE - MARGIN + t, SPAN, stride=STEP), :]
                    if xs_wide is not None:
                        xs_wide[h, r, t] = piece
                    xs[h, r, t] = piece.astype(BF16)
        return 0

    lax.fori_loop(0, rows // 2 + MARGIN, spread, 0)


def stage_cotangent(cot_ref, sea_ref, slot_ref, slots, cot_wide, mask_wide):
    rows, tile, _ = cot_ref.shape
    open_cells = (sea_ref[...] > 0) & (slot_ref[...] < slots)
    mask = jnp.where(open_cells, 1.0, 0.0).astype(F32)
    mask = jnp.concatenate([mask, jnp.zeros((HALF - rows, tile), F32)], axis=0).T
    for r in range(rows):
        column = jnp.broadcast_to(mask[:, r : r + 1], (tile, HALF))
        mask_wide[r] = column
        for h in range(2):
            cot_wide[h, r] = cot_ref[r, :, h * HALF : (h + 1) * HALF].astype(F32) * column


def conv_part(xs, w_ref, h, pair, i2, first, last):
    pieces = []
    for j in range(first, last):
        for a in range(2):
            pieces.append(xs[h, 2 * pair + 2 * i2 + a, j : j + STEP].reshape(STEP * SPAN, HALF))
    span = slice((i2 * KS + first) * 256, (i2 * KS + last) * 256)
    return dot(jnp.concatenate(pieces, axis=1), w_ref[h, span])


def conv_pair(xs, w_ref, h, pair):
    total = conv_part(xs, w_ref, h, pair, 0, 0, KS)
    for i2 in range(1, (KS + 1) // 2):
        total = total + conv_part(xs, w_ref, h, pair, i2, 0, KS)
    return total


def conv_group(xs, w_ref, h, pair):
    pieces = []
    for i2 in range((KS + 1) // 2):
        for j in range(KS):
            for a in range(2):
                rows = [2 * (pair + n) + 2 * i2 + a for n in range(GROUP)]
                pieces.append(
                    jnp.concatenate(
                        [xs[h, r, j : j + STEP].reshape(STEP * SPAN, HALF) for r in rows], axis=0
                    )
                )
    return dot(jnp.concatenate(pieces, axis=1), w_ref[h])


def tap_part(gm_xs, xs_wide, h, i, b, side, pair, sums):
    source = jnp.maximum(pair, 0)
    part = slice(side * 8, side * 8 + 8)
    grads = [gm_xs[h, 2 * pair + 2 + b, t, part] for t in range(STEP)]
    for spot in range(STEP + KS - 1):
        cell = xs_wide[h, 2 * source + b + i, spot, part]
        for j in range(KS):
            if 0 <= spot - j < STEP:
                sums[j] = sums[j] + grads[spot - j] * cell
    return sums


def add_taps(gm_xs, xs_wide, acc_taps, h, i, pair):
    sums = [acc_taps[h, i * KS + j] for j in range(KS)]
    for b in range(2):
        for side in range(2):
            sums = tap_part(gm_xs, xs_wide, h, i, b, side, pair, sums)
    for j in range(KS):
        acc_taps[h, i * KS + j] = sums[j]


def zipped(*lists):
    spots = [((k + 0.5) / len(items), n, k) for n, items in enumerate(lists) for k in range(len(items))]
    return [lists[n][k] for _, n, k in sorted(spots)]


def strided(ref, row):
    return jnp.concatenate(
        [ref[row, pl.ds(t, SPAN, stride=STEP), :] for t in range(STEP)], axis=0
    )


def pack_sums(targets, acc_in, acc_out, acc_scale, acc_taps):
    half_ff = acc_in.shape[1] // 2
    spots = targets[0].shape[0]

    def pack(quad, _):
        for g in range(4):
            group = 4 * quad + g
            for target, acc in zip(targets, (acc_in, acc_out)):
                for side in range(2):
                    target[group * 2 + side, :, 0:half_ff] = acc[
                        pl.ds(pl.multiple_of(group * 8, 8), 8),
                        side * half_ff : (side + 1) * half_ff,
                    ].astype(BF16)
        return 0

    lax.fori_loop(0, spots // 8, pack, 0)
    for spot in range(2 * spots):
        tap, h = spot // 2, spot % 2
        if tap < KS * KS:
            value = acc_taps[h, tap]
        elif tap == KS * KS:
            value = acc_scale[:, h * HALF : (h + 1) * HALF]
        else:
            value = jnp.zeros((8, HALF), F32)
        targets[spot // spots][spot % spots, :, half_ff:] = value.astype(BF16)


def forward_kernel(
    main_ref,
    near_ref,
    far_ref,
    south_ref,
    north_ref,
    cot_ref,
    sea_ref,
    slot_ref,
    taps_ref,
    gain_ref,
    bias_ref,
    w_in_ref,
    b_in_ref,
    w_out_ref,
    scale_ref,
    out_ref,
    gm_ref,
    keep_ref,
    send_ref,
    wide,
    xs,
    xs_wide,
    w_ref,
    out_wide,
    gm_wide,
    gm_xs,
    mask_wide,
    mixed_ref,
    acc_taps,
    acc_in,
    acc_out,
    acc_scale,
):
    rows = main_ref.shape[0]
    ff = w_in_ref.shape[1]
    width = 2 * HALF
    cells = 2 * STEP * SPAN
    build_weights(taps_ref, w_ref, False)
    assemble(main_ref, near_ref, far_ref, south_ref, north_ref, wide, xs, xs_wide)
    stage_cotangent(cot_ref, sea_ref, slot_ref, SLOTS, out_wide, mask_wide)
    acc_in[...] = jnp.zeros_like(acc_in)
    acc_out[...] = jnp.zeros_like(acc_out)
    acc_scale[...] = jnp.zeros_like(acc_scale)
    gain, bias, scale = gain_ref[...], bias_ref[...], scale_ref[...]

    acc_taps[...] = jnp.zeros_like(acc_taps)
    for h in range(2):
        gm_xs[h, 0:2] = jnp.zeros((2, STEP, SPAN, HALF), F32)
        mixed_ref[h] = conv_pair(xs, w_ref, h, 0)

    def finish(pair):
        for row in (2 * pair, 2 * pair + 1):
            for h in range(2):
                lanes = slice(h * HALF, (h + 1) * HALF)
                out_ref[row, :, lanes] = out_wide[h, row].astype(BF16)
                gm_ref[row, :, lanes] = gm_wide[h, row].astype(BF16)

    def pair_step(pair, _):
        finish(jnp.maximum(pair - 1, 0))
        low, high = mixed_ref[0], mixed_ref[1]
        mixed = jnp.concatenate(
            [
                jnp.concatenate([low[:, :HALF], high[:, :HALF]], axis=1),
                jnp.concatenate([low[:, HALF:], high[:, HALF:]], axis=1),
            ],
            axis=0,
        )
        later = jnp.minimum(pair + 1, rows // 2 - 1)
        conv_tasks, sum_tasks = [], []
        for h in range(2):
            begun = {}

            def conv_task(h, i2, first, last, begun):
                part = conv_part(xs, w_ref, h, later, i2, first, last)
                begun[0] = part if 0 not in begun else begun[0] + part
                if i2 == (KS - 1) // 2 and last == KS:
                    mixed_ref[h] = begun[0]

            for i2 in range((KS + 1) // 2):
                for first, last in CUTS:
                    conv_tasks.append(functools.partial(conv_task, h, i2, first, last, begun))
            for i in range(KS):
                sum_tasks.append(
                    functools.partial(add_taps, gm_xs, xs_wide, acc_taps, h, i, pair - 1)
                )
        for work in zipped(conv_tasks, sum_tasks):
            work()
        mean = jnp.mean(mixed, axis=1, keepdims=True)
        centered = mixed - mean
        var = jnp.mean(centered * centered, axis=1, keepdims=True)
        inverse = lax.rsqrt(var + EPSILON)
        normed = centered * inverse
        normalized = (normed * gain + bias).astype(BF16)
        cot = jnp.concatenate(
            [
                jnp.concatenate([strided(out_wide.at[h], 2 * pair + b) for b in range(2)], axis=0)
                for h in range(2)
            ],
            axis=1,
        )
        grad_out = (cot * scale).astype(BF16)
        branch = jnp.zeros((cells, width), F32)
        grad_norm = jnp.zeros((cells, width), F32)
        normalized_t = normalized.T
        grad_out_t = grad_out.T
        parts = ff // 256
        def enter(f):
            part = slice(f * 256, (f + 1) * 256)
            return (
                dot(normalized, w_in_ref[:, part]) + b_in_ref[:, part],
                dot_flipped(grad_out, w_out_ref[part, :]),
            )

        ahead = enter(0)
        for f in range(parts):
            part = slice(f * 256, (f + 1) * 256)
            hidden, grad_act = ahead
            if f + 1 < parts:
                ahead = enter(f + 1)
            square = hidden * hidden
            hyper = jnp.tanh(hidden * (GELU_SCALE + GELU_SCALE * GELU_CUBE * square))
            gate = 0.5 + 0.5 * hyper
            act = hidden * gate
            slope = gate + act * (1.0 - gate) * (
                2.0 * GELU_SCALE + 6.0 * GELU_SCALE * GELU_CUBE * square
            )
            act_low = act.astype(BF16)
            grad_hidden = (grad_act * slope).astype(BF16)
            branch = branch + dot(act_low, w_out_ref[part, :])
            grad_norm = grad_norm + dot_flipped(grad_hidden, w_in_ref[:, part])
            acc_in[:, part] += dot(normalized_t, grad_hidden)
            acc_out[:, part] += dot(grad_out_t, act_low)
        branch = branch.astype(BF16).astype(F32)
        acc_scale[...] += jnp.sum((cot * branch).reshape(cells // 8, 8, width), axis=0)
        g = grad_norm.astype(BF16).astype(F32) * gain
        grad_mixed = inverse * (
            g
            - jnp.mean(g, axis=1, keepdims=True)
            - normed * jnp.mean(g * normed, axis=1, keepdims=True)
        )
        grad_mixed = grad_mixed.astype(BF16).astype(F32)
        mask = jnp.concatenate([strided(mask_wide, 2 * pair + b) for b in range(2)], axis=0)
        for h in range(2):
            lanes = slice(h * HALF, (h + 1) * HALF)
            added = mask * scale[:, lanes] * branch[:, lanes]
            for b in range(2):
                row = 2 * pair + b
                for t in range(STEP):
                    start = b * STEP * SPAN + t * SPAN
                    feature = xs_wide[h, row + MARGIN, t + MARGIN]
                    out_wide[h, row, pl.ds(t, SPAN, stride=STEP), :] = (
                        feature + added[start : start + SPAN]
                    )
                    piece = grad_mixed[start : start + SPAN, lanes]
                    gm_wide[h, row, pl.ds(t, SPAN, stride=STEP), :] = piece
                    gm_xs[h, row + 2, t] = piece
        return 0

    lax.fori_loop(0, rows // 2, pair_step, 0)

    finish(rows // 2 - 1)
    for h in range(2):
        for i in range(KS):
            add_taps(gm_xs, xs_wide, acc_taps, h, i, rows // 2 - 1)
    core = lax.axis_index("core")

    @pl.when(core == 0)
    def _():
        pack_sums((keep_ref, send_ref), acc_in, acc_out, acc_scale, acc_taps)

    @pl.when(core != 0)
    def _():
        pack_sums((send_ref, keep_ref), acc_in, acc_out, acc_scale, acc_taps)


def backward_kernel(
    main_ref,
    near_ref,
    far_ref,
    south_ref,
    north_ref,
    cot_ref,
    taps_ref,
    out_ref,
    wide,
    xs,
    w_ref,
    out_wide,
):
    rows = main_ref.shape[0]
    build_weights(taps_ref, w_ref, True)
    assemble(main_ref, near_ref, far_ref, south_ref, north_ref, wide, xs)

    def finish(group, h):
        lanes = slice(h * HALF, (h + 1) * HALF)
        for b in range(2 * GROUP):
            row = 2 * GROUP * group + b
            out_ref[row, :, lanes] = (
                cot_ref[row, :, lanes].astype(F32) + out_wide[h, row]
            ).astype(BF16)

    def group_step(group, _):
        for h in range(2):
            both = conv_group(xs, w_ref, h, GROUP * group)
            for n in range(GROUP):
                for b in range(2):
                    for t in range(STEP):
                        start = (n * STEP + t) * SPAN
                        row = 2 * (GROUP * group + n) + b
                        out_wide[h, row, pl.ds(t, SPAN, stride=STEP), :] = both[
                            start : start + SPAN, b * HALF : (b + 1) * HALF
                        ]
            finish(group, h)
        return 0

    lax.fori_loop(0, rows // 2 // GROUP, group_step, 0)


def rim_sides(field):
    tile = field.shape[1]
    even = lax.axis_index("core") == 0
    low, high = field[:, :EDGE], field[:, tile - EDGE :]
    count = lax.axis_size(LON)
    across = [(i, (i + 1) % count) for i in range(1, count, 2)]
    across += [(target, source) for source, target in across]
    far = lax.ppermute(jnp.where(even, low, high), LON, across)
    near = lax.ppermute(jnp.where(even, high, low), "core", [(0, 1), (1, 0)])
    return near, far


def rim_messages(field, near, far):
    rows = field.shape[0]
    even = lax.axis_index("core") == 0

    def across(part):
        west = jnp.where(even, far[part], near[part])
        east = jnp.where(even, near[part], far[part])
        return jnp.concatenate([west, field[part], east], axis=1)

    return across(slice(rows - MARGIN, rows)), across(slice(0, MARGIN))


def rim_ends(up, down):
    count = lax.axis_size(LAT)
    forward = [(i, (i + 1) % count) for i in range(count)]
    backward = [(i, (i - 1) % count) for i in range(count)]
    return lax.ppermute(up, LAT, forward), lax.ppermute(down, LAT, backward)


def on_device(
    features, cotangent, land_sea, tile_slot, kernel, ln_gain, ln_bias, w_in, b_in, w_out, layer_scale
):
    rows, tile, width = features.shape
    ff = w_in.shape[1]
    chips = lax.axis_size(CHIPS)
    padded = rows + 2 * MARGIN
    ext = STEP + 2 * MARGIN
    vmem = pl.BlockSpec(memory_space=pltpu.VMEM)
    wide = pltpu.VMEM((2, padded, tile + 2 * EDGE, HALF), F32)
    xs = pltpu.VMEM((2, padded, ext, SPAN, HALF), BF16)
    weights = pltpu.VMEM((2, TAPS * 256, 256), BF16)
    flat = pltpu.VMEM((2, rows, tile, HALF), F32)
    near, far = rim_sides(features)
    south, north = rim_ends(*rim_messages(features, near, far))
    chunk = ff // 2 + HALF
    output, grad_mixed, keep, send = pl.pallas_call(
        forward_kernel,
        out_shape=(
            jax.ShapeDtypeStruct(features.shape, BF16),
            jax.ShapeDtypeStruct(features.shape, BF16),
            jax.ShapeDtypeStruct((chips, 8, chunk), BF16),
            jax.ShapeDtypeStruct((chips, 8, chunk), BF16),
        ),
        in_specs=[vmem] * 15,
        out_specs=(vmem,) * 4,
        scratch_shapes=[
            wide,
            xs,
            pltpu.VMEM((2, padded, ext, SPAN, HALF), F32),
            weights,
            flat,
            flat,
            pltpu.VMEM((2, rows + 2, STEP, SPAN, HALF), F32),
            pltpu.VMEM((rows, tile, HALF), F32),
            pltpu.VMEM((2, STEP * SPAN, 256), F32),
            pltpu.VMEM((2, KS * KS, 8, HALF), F32),
            pltpu.VMEM((width, ff), F32),
            pltpu.VMEM((width, ff), F32),
            pltpu.VMEM((8, width), F32),
        ],
        compiler_params=pltpu.CompilerParams(vmem_limit_bytes=FORWARD_VMEM),
        cost_estimate=pl.CostEstimate(
            flops=14_000_000_000, bytes_accessed=8_000_000, transcendentals=2_000_000
        ),
        name="forward",
    )(
        features,
        near,
        far,
        south,
        north,
        cotangent,
        land_sea,
        tile_slot,
        kernel,
        ln_gain.reshape(1, width),
        ln_bias.reshape(1, width),
        w_in,
        b_in.reshape(1, ff),
        w_out,
        layer_scale.reshape(1, width),
    )
    swap = [(0, 1), (1, 0)]
    sums = (keep.astype(F32) + lax.ppermute(send, "core", swap).astype(F32)).astype(BF16)
    sums, grad_mixed = lax.optimization_barrier((sums, grad_mixed))
    near, far = rim_sides(grad_mixed)
    south, north = rim_ends(*rim_messages(grad_mixed, near, far))
    arrived = lax.all_to_all(sums, CHIPS, split_axis=0, concat_axis=0, tiled=True)
    own, grad_mixed, near, far, south, north = lax.optimization_barrier(
        (
            jnp.sum(arrived.astype(F32), axis=0).astype(BF16),
            grad_mixed,
            near,
            far,
            south,
            north,
        )
    )
    mine = lax.all_to_all(
        jnp.broadcast_to(own[None], (chips,) + own.shape), CHIPS, split_axis=0, concat_axis=0, tiled=True
    )
    grad_features = pl.pallas_call(
        backward_kernel,
        out_shape=jax.ShapeDtypeStruct(features.shape, BF16),
        in_specs=[vmem] * 7,
        out_specs=vmem,
        scratch_shapes=[wide, xs, weights, flat],
        compiler_params=pltpu.CompilerParams(vmem_limit_bytes=BACKWARD_VMEM),
        cost_estimate=pl.CostEstimate(
            flops=7_000_000_000, bytes_accessed=4_000_000, transcendentals=0
        ),
        name="backward",
    )(grad_mixed, near, far, south, north, cotangent, kernel)
    mine, grad_features = lax.optimization_barrier((mine, grad_features))
    other = lax.ppermute(mine, "core", swap)
    factor = 1.0 / math.sqrt(rows * lax.axis_size(LAT) * tile * lax.axis_size(LON))
    grad_in, grad_out, grad_taps, grad_scale = pl.pallas_call(
        functools.partial(unpack_kernel, factor),
        out_shape=(
            jax.ShapeDtypeStruct((width, ff), F32),
            jax.ShapeDtypeStruct((ff, width), F32),
            jax.ShapeDtypeStruct(kernel.shape, F32),
            jax.ShapeDtypeStruct((1, width), F32),
        ),
        in_specs=[vmem] * 2,
        out_specs=(vmem,) * 4,
        compiler_params=pltpu.CompilerParams(vmem_limit_bytes=BACKWARD_VMEM),
        name="unpack",
    )(mine, other)
    return (
        output,
        grad_features,
        grad_in,
        grad_out,
        grad_taps,
        grad_scale.reshape(width),
    )


def unpack_kernel(factor, mine_ref, other_ref, grad_in_ref, grad_out_ref, taps_ref, scale_ref):
    half_ff = grad_in_ref.shape[1] // 2
    spots = mine_ref.shape[0]

    def unpack(first_ref, second_ref):
        def quad(n, _):
            for g in range(2):
                for side in range(2):
                    group = 2 * n + g
                    columns = slice(side * half_ff, (side + 1) * half_ff)
                    grad_in_ref[pl.ds(pl.multiple_of(group * 8, 8), 8), columns] = (
                        first_ref[group * 2 + side, :, :half_ff].astype(F32) * factor
                    )
            return 0

        lax.fori_loop(0, spots // 4, quad, 0)
        for block in range(grad_out_ref.shape[1] // HALF):
            for side in range(2):
                rows = [
                    second_ref[(block * SPAN + n) * 2 + side, :, :half_ff].astype(F32)
                    for n in range(SPAN)
                ]
                grad_out_ref[
                    side * half_ff : (side + 1) * half_ff, block * HALF : (block + 1) * HALF
                ] = jnp.concatenate(rows, axis=0).T * factor
        for spot in range(2 * (KS * KS + 1)):
            ref = first_ref if spot < spots else second_ref
            tap, h = spot // 2, spot % 2
            part = ref[spot % spots, :, half_ff:].astype(F32)
            lanes = slice(h * HALF, (h + 1) * HALF)
            total = jnp.sum(part, axis=0, keepdims=True) * factor
            if tap < KS * KS:
                taps_ref[tap // KS, tap % KS : tap % KS + 1, lanes] = total
            else:
                scale_ref[:, lanes] = total

    core = lax.axis_index("core")

    @pl.when(core == 0)
    def _():
        unpack(mine_ref, other_ref)

    @pl.when(core != 0)
    def _():
        unpack(other_ref, mine_ref)


def solution(mesh):
    fine = Mesh(mesh.devices.reshape(4, 2, 2, 2, 4), ("x", "zh", "core", "zl", "y"))
    cells = P(LAT, LON, None)
    return jax.shard_map(
        on_device,
        mesh=fine,
        in_specs=(cells, cells, P(LAT, LON), P(LAT, LON)) + (P(),) * 7,
        out_specs=(cells, cells, P(), P(), P(), P()),
        check_vma=False,
    )
```

```python
import functools
import math

import jax
import jax.numpy as jnp
from jax import lax
from jax.experimental import pallas as pl
from jax.experimental.pallas import tpu as pltpu
from jax.sharding import Mesh
from jax.sharding import PartitionSpec as P

KS = 7
MARGIN = KS // 2
HALF = 128
STEP = 8
SPAN = 16
EDGE = 8
SLOTS = 64
FORWARD_VMEM = 51 * 1024 * 1024
BACKWARD_VMEM = 28 * 1024 * 1024
GROUP = 4
CUTS = ((0, 2), (2, 4), (4, 7))
TAPS = (KS + 1) // 2 * KS
GELU_SCALE = math.sqrt(2.0 / math.pi)
GELU_CUBE = 0.044715
EPSILON = 1e-06
LON = ("x", "zh", "core")
LAT = ("zl", "y")
CHIPS = ("x", "zh", "zl", "y")
ALL = ("x", "zh", "core", "zl", "y")
F32 = jnp.float32
BF16 = jnp.bfloat16


def dot(a, b):
    return jnp.dot(a, b, preferred_element_type=F32)


def dot_flipped(a, b):
    return lax.dot_general(a, b, (((1,), (1,)), ((), ())), preferred_element_type=F32)


def build_weights(taps_ref, w_ref, flip):
    rows = lax.broadcasted_iota(jnp.int32, (HALF, HALF), 0)
    cols = lax.broadcasted_iota(jnp.int32, (HALF, HALF), 1)
    eye = rows == cols
    zero = jnp.zeros((HALF, HALF), F32)
    for h in range(2):
        for i2 in range((KS + 1) // 2):
            for j in range(KS):
                tile = i2 * KS + j
                for a in range(2):
                    for b in range(2):
                        i = 2 * i2 + a - b
                        if 0 <= i < KS:
                            tap = (KS - 1 - i) * KS + (KS - 1 - j) if flip else i * KS + j
                            row = taps_ref[tap // KS, tap % KS : tap % KS + 1, h * HALF : (h + 1) * HALF]
                            block = jnp.where(eye, row, zero)
                        else:
                            block = zero
                        w_ref[
                            h,
                            tile * 256 + a * HALF : tile * 256 + (a + 1) * HALF,
                            b * HALF : (b + 1) * HALF,
                        ] = block.astype(BF16)


def assemble(main_ref, near_ref, far_ref, south_ref, north_ref, wide, xs, xs_wide=None):
    rows, tile, _ = main_ref.shape
    even = lax.axis_index("core") == 0
    band = lax.axis_index(LAT)
    below = jnp.where(band > 0, 1.0, 0.0).astype(F32)
    above = jnp.where(band < lax.axis_size(LAT) - 1, 1.0, 0.0).astype(F32)
    for h in range(2):
        lanes = slice(h * HALF, (h + 1) * HALF)
        wide[h, 0:MARGIN] = south_ref[:, :, lanes].astype(F32) * below
        wide[h, rows + MARGIN : rows + 2 * MARGIN] = north_ref[:, :, lanes].astype(F32) * above

    def place(pair, _):
        for r in (2 * pair, 2 * pair + 1):
            for h in range(2):
                lanes = slice(h * HALF, (h + 1) * HALF)
                wide[h, r + MARGIN, EDGE : EDGE + tile, :] = main_ref[r, :, lanes].astype(F32)
                near = near_ref[r, :, lanes].astype(F32)
                far = far_ref[r, :, lanes].astype(F32)
                wide[h, r + MARGIN, 0:EDGE, :] = jnp.where(even, far, near)
                wide[h, r + MARGIN, EDGE + tile : 2 * EDGE + tile, :] = jnp.where(even, near, far)
        return 0

    lax.fori_loop(0, rows // 2, place, 0)

    def spread(pair, _):
        for r in (2 * pair, 2 * pair + 1):
            for h in range(2):
                for t in range(STEP + 2 * MARGIN):
                    piece = wide[h, r, pl.ds(EDGE - MARGIN + t, SPAN, stride=STEP), :]
                    if xs_wide is not None:
                        xs_wide[h, r, t] = piece
                    xs[h, r, t] = piece.astype(BF16)
        return 0

    lax.fori_loop(0, rows // 2 + MARGIN, spread, 0)


def stage_cotangent(cot_ref, sea_ref, slot_ref, slots, cot_wide, mask_wide):
    rows, tile, _ = cot_ref.shape
    open_cells = (sea_ref[...] > 0) & (slot_ref[...] < slots)
    mask = jnp.where(open_cells, 1.0, 0.0).astype(F32)
    mask = jnp.concatenate([mask, jnp.zeros((HALF - rows, tile), F32)], axis=0).T
    for r in range(rows):
        column = jnp.broadcast_to(mask[:, r : r + 1], (tile, HALF))
        mask_wide[r] = column
        for h in range(2):
            cot_wide[h, r] = cot_ref[r, :, h * HALF : (h + 1) * HALF].astype(F32) * column


def conv_part(xs, w_ref, h, pair, i2, first, last):
    pieces = []
    for j in range(first, last):
        for a in range(2):
            pieces.append(xs[h, 2 * pair + 2 * i2 + a, j : j + STEP].reshape(STEP * SPAN, HALF))
    span = slice((i2 * KS + first) * 256, (i2 * KS + last) * 256)
    return dot(jnp.concatenate(pieces, axis=1), w_ref[h, span])


def conv_pair(xs, w_ref, h, pair):
    total = conv_part(xs, w_ref, h, pair, 0, 0, KS)
    for i2 in range(1, (KS + 1) // 2):
        total = total + conv_part(xs, w_ref, h, pair, i2, 0, KS)
    return total


def conv_group(xs, w_ref, h, pair):
    pieces = []
    for i2 in range((KS + 1) // 2):
        for j in range(KS):
            for a in range(2):
                rows = [2 * (pair + n) + 2 * i2 + a for n in range(GROUP)]
                pieces.append(
                    jnp.concatenate(
                        [xs[h, r, j : j + STEP].reshape(STEP * SPAN, HALF) for r in rows], axis=0
                    )
                )
    return dot(jnp.concatenate(pieces, axis=1), w_ref[h])


def tap_part(gm_xs, xs_wide, h, i, b, side, pair, sums):
    source = jnp.maximum(pair, 0)
    part = slice(side * 8, side * 8 + 8)
    grads = [gm_xs[h, 2 * pair + 2 + b, t, part] for t in range(STEP)]
    for spot in range(STEP + KS - 1):
        cell = xs_wide[h, 2 * source + b + i, spot, part]
        for j in range(KS):
            if 0 <= spot - j < STEP:
                sums[j] = sums[j] + grads[spot - j] * cell
    return sums


def add_taps(gm_xs, xs_wide, acc_taps, h, i, pair):
    sums = [acc_taps[h, i * KS + j] for j in range(KS)]
    for b in range(2):
        for side in range(2):
            sums = tap_part(gm_xs, xs_wide, h, i, b, side, pair, sums)
    for j in range(KS):
        acc_taps[h, i * KS + j] = sums[j]


def zipped(*lists):
    spots = [((k + 0.5) / len(items), n, k) for n, items in enumerate(lists) for k in range(len(items))]
    return [lists[n][k] for _, n, k in sorted(spots)]


def strided(ref, row):
    return jnp.concatenate(
        [ref[row, pl.ds(t, SPAN, stride=STEP), :] for t in range(STEP)], axis=0
    )


def pack_sums(targets, acc_in, acc_out, acc_scale, acc_taps):
    half_ff = acc_in.shape[1] // 2
    spots = targets[0].shape[0]

    def pack(quad, _):
        for g in range(4):
            group = 4 * quad + g
            for target, acc in zip(targets, (acc_in, acc_out)):
                for side in range(2):
                    target[group * 2 + side, :, 0:half_ff] = acc[
                        pl.ds(pl.multiple_of(group * 8, 8), 8),
                        side * half_ff : (side + 1) * half_ff,
                    ].astype(BF16)
        return 0

    lax.fori_loop(0, spots // 8, pack, 0)
    for spot in range(2 * spots):
        tap, h = spot // 2, spot % 2
        if tap < KS * KS:
            value = acc_taps[h, tap]
        elif tap == KS * KS:
            value = acc_scale[:, h * HALF : (h + 1) * HALF]
        else:
            value = jnp.zeros((8, HALF), F32)
        targets[spot // spots][spot % spots, :, half_ff:] = value.astype(BF16)


def forward_kernel(
    main_hbm,
    near_ref,
    far_ref,
    south_ref,
    north_ref,
    cot_hbm,
    sea_ref,
    slot_ref,
    taps_ref,
    gain_ref,
    bias_ref,
    w_in_hbm,
    b_in_ref,
    w_out_hbm,
    scale_ref,
    out_hbm,
    gm_hbm,
    keep_ref,
    send_ref,
    wide,
    xs,
    xs_wide,
    w_ref,
    out_wide,
    gm_wide,
    gm_xs,
    mask_wide,
    mixed_ref,
    acc_taps,
    acc_in,
    acc_out,
    acc_scale,
    main_ref,
    cot_ref,
    w_in_ref,
    w_out_ref,
    out_ref,
    gm_ref,
    sems,
):
    moves = [
        pltpu.make_async_copy(source, target, sems.at[n])
        for n, (source, target) in enumerate(
            (
                (main_hbm, main_ref),
                (cot_hbm, cot_ref),
                (w_in_hbm, w_in_ref),
                (w_out_hbm, w_out_ref),
                (gm_ref, gm_hbm),
                (out_ref, out_hbm),
            )
        )
    ]
    for move in moves[:4]:
        move.start()
    rows = main_ref.shape[0]
    ff = w_in_ref.shape[1]
    width = 2 * HALF
    cells = 2 * STEP * SPAN
    build_weights(taps_ref, w_ref, False)
    moves[0].wait()
    assemble(main_ref, near_ref, far_ref, south_ref, north_ref, wide, xs, xs_wide)
    moves[1].wait()
    stage_cotangent(cot_ref, sea_ref, slot_ref, SLOTS, out_wide, mask_wide)
    acc_in[...] = jnp.zeros_like(acc_in)
    acc_out[...] = jnp.zeros_like(acc_out)
    acc_scale[...] = jnp.zeros_like(acc_scale)
    gain, bias, scale = gain_ref[...], bias_ref[...], scale_ref[...]

    moves[2].wait()
    moves[3].wait()
    acc_taps[...] = jnp.zeros_like(acc_taps)
    for h in range(2):
        gm_xs[h, 0:2] = jnp.zeros((2, STEP, SPAN, HALF), F32)
        mixed_ref[h] = conv_pair(xs, w_ref, h, 0)

    def finish(pair):
        for row in (2 * pair, 2 * pair + 1):
            for h in range(2):
                lanes = slice(h * HALF, (h + 1) * HALF)
                out_ref[row, :, lanes] = out_wide[h, row].astype(BF16)
                gm_ref[row, :, lanes] = gm_wide[h, row].astype(BF16)

    def pair_step(pair, _):
        finish(jnp.maximum(pair - 1, 0))
        low, high = mixed_ref[0], mixed_ref[1]
        mixed = jnp.concatenate(
            [
                jnp.concatenate([low[:, :HALF], high[:, :HALF]], axis=1),
                jnp.concatenate([low[:, HALF:], high[:, HALF:]], axis=1),
            ],
            axis=0,
        )
        later = jnp.minimum(pair + 1, rows // 2 - 1)
        conv_tasks, sum_tasks = [], []
        for h in range(2):
            begun = {}

            def conv_task(h, i2, first, last, begun):
                part = conv_part(xs, w_ref, h, later, i2, first, last)
                begun[0] = part if 0 not in begun else begun[0] + part
                if i2 == (KS - 1) // 2 and last == KS:
                    mixed_ref[h] = begun[0]

            for i2 in range((KS + 1) // 2):
                for first, last in CUTS:
                    conv_tasks.append(functools.partial(conv_task, h, i2, first, last, begun))
            for i in range(KS):
                sum_tasks.append(
                    functools.partial(add_taps, gm_xs, xs_wide, acc_taps, h, i, pair - 1)
                )
        for work in zipped(conv_tasks, sum_tasks):
            work()
        mean = jnp.mean(mixed, axis=1, keepdims=True)
        centered = mixed - mean
        var = jnp.mean(centered * centered, axis=1, keepdims=True)
        inverse = lax.rsqrt(var + EPSILON)
        normed = centered * inverse
        normalized = (normed * gain + bias).astype(BF16)
        cot = jnp.concatenate(
            [
                jnp.concatenate([strided(out_wide.at[h], 2 * pair + b) for b in range(2)], axis=0)
                for h in range(2)
            ],
            axis=1,
        )
        grad_out = (cot * scale).astype(BF16)
        branch = jnp.zeros((cells, width), F32)
        grad_norm = jnp.zeros((cells, width), F32)
        normalized_t = normalized.T
        grad_out_t = grad_out.T
        parts = ff // 256
        def enter(f):
            part = slice(f * 256, (f + 1) * 256)
            return (
                dot(normalized, w_in_ref[:, part]) + b_in_ref[:, part],
                dot_flipped(grad_out, w_out_ref[part, :]),
            )

        ahead = enter(0)
        for f in range(parts):
            part = slice(f * 256, (f + 1) * 256)
            hidden, grad_act = ahead
            if f + 1 < parts:
                ahead = enter(f + 1)
            square = hidden * hidden
            hyper = jnp.tanh(hidden * (GELU_SCALE + GELU_SCALE * GELU_CUBE * square))
            gate = 0.5 + 0.5 * hyper
            act = hidden * gate
            slope = gate + act * (1.0 - gate) * (
                2.0 * GELU_SCALE + 6.0 * GELU_SCALE * GELU_CUBE * square
            )
            act_low = act.astype(BF16)
            grad_hidden = (grad_act * slope).astype(BF16)
            branch = branch + dot(act_low, w_out_ref[part, :])
            grad_norm = grad_norm + dot_flipped(grad_hidden, w_in_ref[:, part])
            acc_in[:, part] += dot(normalized_t, grad_hidden)
            acc_out[:, part] += dot(grad_out_t, act_low)
        branch = branch.astype(BF16).astype(F32)
        acc_scale[...] += jnp.sum((cot * branch).reshape(cells // 8, 8, width), axis=0)
        g = grad_norm.astype(BF16).astype(F32) * gain
        grad_mixed = inverse * (
            g
            - jnp.mean(g, axis=1, keepdims=True)
            - normed * jnp.mean(g * normed, axis=1, keepdims=True)
        )
        grad_mixed = grad_mixed.astype(BF16).astype(F32)
        mask = jnp.concatenate([strided(mask_wide, 2 * pair + b) for b in range(2)], axis=0)
        for h in range(2):
            lanes = slice(h * HALF, (h + 1) * HALF)
            added = mask * scale[:, lanes] * branch[:, lanes]
            for b in range(2):
                row = 2 * pair + b
                for t in range(STEP):
                    start = b * STEP * SPAN + t * SPAN
                    feature = xs_wide[h, row + MARGIN, t + MARGIN]
                    out_wide[h, row, pl.ds(t, SPAN, stride=STEP), :] = (
                        feature + added[start : start + SPAN]
                    )
                    piece = grad_mixed[start : start + SPAN, lanes]
                    gm_wide[h, row, pl.ds(t, SPAN, stride=STEP), :] = piece
                    gm_xs[h, row + 2, t] = piece
        return 0

    lax.fori_loop(0, rows // 2, pair_step, 0)

    finish(rows // 2 - 1)
    moves[4].start()
    moves[5].start()
    for h in range(2):
        for i in range(KS):
            add_taps(gm_xs, xs_wide, acc_taps, h, i, rows // 2 - 1)
    core = lax.axis_index("core")

    @pl.when(core == 0)
    def _():
        pack_sums((keep_ref, send_ref), acc_in, acc_out, acc_scale, acc_taps)

    @pl.when(core != 0)
    def _():
        pack_sums((send_ref, keep_ref), acc_in, acc_out, acc_scale, acc_taps)

    moves[4].wait()
    moves[5].wait()


def backward_kernel(
    main_ref,
    near_ref,
    far_ref,
    south_ref,
    north_ref,
    cot_ref,
    taps_ref,
    out_ref,
    wide,
    xs,
    w_ref,
    out_wide,
):
    rows = main_ref.shape[0]
    build_weights(taps_ref, w_ref, True)
    assemble(main_ref, near_ref, far_ref, south_ref, north_ref, wide, xs)

    def finish(group, h):
        lanes = slice(h * HALF, (h + 1) * HALF)
        for b in range(2 * GROUP):
            row = 2 * GROUP * group + b
            out_ref[row, :, lanes] = (
                cot_ref[row, :, lanes].astype(F32) + out_wide[h, row]
            ).astype(BF16)

    def group_step(group, _):
        for h in range(2):
            both = conv_group(xs, w_ref, h, GROUP * group)
            for n in range(GROUP):
                for b in range(2):
                    for t in range(STEP):
                        start = (n * STEP + t) * SPAN
                        row = 2 * (GROUP * group + n) + b
                        out_wide[h, row, pl.ds(t, SPAN, stride=STEP), :] = both[
                            start : start + SPAN, b * HALF : (b + 1) * HALF
                        ]
            finish(group, h)
        return 0

    lax.fori_loop(0, rows // 2 // GROUP, group_step, 0)


def rim_sides(field):
    tile = field.shape[1]
    even = lax.axis_index("core") == 0
    low, high = field[:, :EDGE], field[:, tile - EDGE :]
    count = lax.axis_size(LON)
    across = [(i, (i + 1) % count) for i in range(1, count, 2)]
    across += [(target, source) for source, target in across]
    far = lax.ppermute(jnp.where(even, low, high), LON, across)
    near = lax.ppermute(jnp.where(even, high, low), "core", [(0, 1), (1, 0)])
    return near, far


def rim_messages(field, near, far):
    rows = field.shape[0]
    even = lax.axis_index("core") == 0

    def across(part):
        west = jnp.where(even, far[part], near[part])
        east = jnp.where(even, near[part], far[part])
        return jnp.concatenate([west, field[part], east], axis=1)

    return across(slice(rows - MARGIN, rows)), across(slice(0, MARGIN))


def rim_ends(up, down):
    count = lax.axis_size(LAT)
    forward = [(i, (i + 1) % count) for i in range(count)]
    backward = [(i, (i - 1) % count) for i in range(count)]
    return lax.ppermute(up, LAT, forward), lax.ppermute(down, LAT, backward)


def on_device(
    features, cotangent, land_sea, tile_slot, kernel, ln_gain, ln_bias, w_in, b_in, w_out, layer_scale
):
    rows, tile, width = features.shape
    ff = w_in.shape[1]
    chips = lax.axis_size(CHIPS)
    padded = rows + 2 * MARGIN
    ext = STEP + 2 * MARGIN
    vmem = pl.BlockSpec(memory_space=pltpu.VMEM)
    hbm = pl.BlockSpec(memory_space=pl.ANY)
    wide = pltpu.VMEM((2, padded, tile + 2 * EDGE, HALF), F32)
    xs = pltpu.VMEM((2, padded, ext, SPAN, HALF), BF16)
    weights = pltpu.VMEM((2, TAPS * 256, 256), BF16)
    flat = pltpu.VMEM((2, rows, tile, HALF), F32)
    near, far = rim_sides(features)
    south, north = rim_ends(*rim_messages(features, near, far))
    chunk = ff // 2 + HALF
    output, grad_mixed, keep, send = pl.pallas_call(
        forward_kernel,
        out_shape=(
            jax.ShapeDtypeStruct(features.shape, BF16),
            jax.ShapeDtypeStruct(features.shape, BF16),
            jax.ShapeDtypeStruct((chips, 8, chunk), BF16),
            jax.ShapeDtypeStruct((chips, 8, chunk), BF16),
        ),
        in_specs=[hbm] + [vmem] * 4 + [hbm] + [vmem] * 5 + [hbm, vmem, hbm, vmem],
        out_specs=(hbm, hbm, vmem, vmem),
        scratch_shapes=[
            wide,
            xs,
            pltpu.VMEM((2, padded, ext, SPAN, HALF), F32),
            weights,
            flat,
            flat,
            pltpu.VMEM((2, rows + 2, STEP, SPAN, HALF), F32),
            pltpu.VMEM((rows, tile, HALF), F32),
            pltpu.VMEM((2, STEP * SPAN, 256), F32),
            pltpu.VMEM((2, KS * KS, 8, HALF), F32),
            pltpu.VMEM((width, ff), F32),
            pltpu.VMEM((width, ff), F32),
            pltpu.VMEM((8, width), F32),
            pltpu.VMEM(features.shape, BF16),
            pltpu.VMEM(features.shape, BF16),
            pltpu.VMEM(w_in.shape, BF16),
            pltpu.VMEM(w_out.shape, BF16),
            pltpu.VMEM(features.shape, BF16),
            pltpu.VMEM(features.shape, BF16),
            pltpu.SemaphoreType.DMA((6,)),
        ],
        compiler_params=pltpu.CompilerParams(vmem_limit_bytes=FORWARD_VMEM),
        cost_estimate=pl.CostEstimate(
            flops=14_000_000_000, bytes_accessed=8_000_000, transcendentals=2_000_000
        ),
        name="forward",
    )(
        features,
        near,
        far,
        south,
        north,
        cotangent,
        land_sea,
        tile_slot,
        kernel,
        ln_gain.reshape(1, width),
        ln_bias.reshape(1, width),
        w_in,
        b_in.reshape(1, ff),
        w_out,
        layer_scale.reshape(1, width),
    )
    swap = [(0, 1), (1, 0)]
    sums = (keep.astype(F32) + lax.ppermute(send, "core", swap).astype(F32)).astype(BF16)
    sums, grad_mixed = lax.optimization_barrier((sums, grad_mixed))
    near, far = rim_sides(grad_mixed)
    south, north = rim_ends(*rim_messages(grad_mixed, near, far))
    arrived = lax.all_to_all(sums, CHIPS, split_axis=0, concat_axis=0, tiled=True)
    own, grad_mixed, near, far, south, north = lax.optimization_barrier(
        (
            jnp.sum(arrived.astype(F32), axis=0).astype(BF16),
            grad_mixed,
            near,
            far,
            south,
            north,
        )
    )
    mine = lax.all_to_all(
        jnp.broadcast_to(own[None], (chips,) + own.shape), CHIPS, split_axis=0, concat_axis=0, tiled=True
    )
    grad_features = pl.pallas_call(
        backward_kernel,
        out_shape=jax.ShapeDtypeStruct(features.shape, BF16),
        in_specs=[vmem] * 7,
        out_specs=vmem,
        scratch_shapes=[wide, xs, weights, flat],
        compiler_params=pltpu.CompilerParams(vmem_limit_bytes=BACKWARD_VMEM),
        cost_estimate=pl.CostEstimate(
            flops=7_000_000_000, bytes_accessed=4_000_000, transcendentals=0
        ),
        name="backward",
    )(grad_mixed, near, far, south, north, cotangent, kernel)
    mine, grad_features = lax.optimization_barrier((mine, grad_features))
    other = lax.ppermute(mine, "core", swap)
    factor = 1.0 / math.sqrt(rows * lax.axis_size(LAT) * tile * lax.axis_size(LON))
    grad_in, grad_out, grad_taps, grad_scale = pl.pallas_call(
        functools.partial(unpack_kernel, factor),
        out_shape=(
            jax.ShapeDtypeStruct((width, ff), F32),
            jax.ShapeDtypeStruct((ff, width), F32),
            jax.ShapeDtypeStruct(kernel.shape, F32),
            jax.ShapeDtypeStruct((1, width), F32),
        ),
        in_specs=[vmem] * 2,
        out_specs=(vmem,) * 4,
        compiler_params=pltpu.CompilerParams(vmem_limit_bytes=BACKWARD_VMEM),
        name="unpack",
    )(mine, other)
    return (
        output,
        grad_features,
        grad_in,
        grad_out,
        grad_taps,
        grad_scale.reshape(width),
    )


def unpack_kernel(factor, mine_ref, other_ref, grad_in_ref, grad_out_ref, taps_ref, scale_ref):
    half_ff = grad_in_ref.shape[1] // 2
    spots = mine_ref.shape[0]

    def unpack(first_ref, second_ref):
        def quad(n, _):
            for g in range(2):
                for side in range(2):
                    group = 2 * n + g
                    columns = slice(side * half_ff, (side + 1) * half_ff)
                    grad_in_ref[pl.ds(pl.multiple_of(group * 8, 8), 8), columns] = (
                        first_ref[group * 2 + side, :, :half_ff].astype(F32) * factor
                    )
            return 0

        lax.fori_loop(0, spots // 4, quad, 0)
        for block in range(grad_out_ref.shape[1] // HALF):
            for side in range(2):
                rows = [
                    second_ref[(block * SPAN + n) * 2 + side, :, :half_ff].astype(F32)
                    for n in range(SPAN)
                ]
                grad_out_ref[
                    side * half_ff : (side + 1) * half_ff, block * HALF : (block + 1) * HALF
                ] = jnp.concatenate(rows, axis=0).T * factor
        for spot in range(2 * (KS * KS + 1)):
            ref = first_ref if spot < spots else second_ref
            tap, h = spot // 2, spot % 2
            part = ref[spot % spots, :, half_ff:].astype(F32)
            lanes = slice(h * HALF, (h + 1) * HALF)
            total = jnp.sum(part, axis=0, keepdims=True) * factor
            if tap < KS * KS:
                taps_ref[tap // KS, tap % KS : tap % KS + 1, lanes] = total
            else:
                scale_ref[:, lanes] = total

    core = lax.axis_index("core")

    @pl.when(core == 0)
    def _():
        unpack(mine_ref, other_ref)

    @pl.when(core != 0)
    def _():
        unpack(other_ref, mine_ref)


def solution(mesh):
    fine = Mesh(mesh.devices.reshape(4, 2, 2, 2, 4), ("x", "zh", "core", "zl", "y"))
    cells = P(LAT, LON, None)
    return jax.shard_map(
        on_device,
        mesh=fine,
        in_specs=(cells, cells, P(LAT, LON), P(LAT, LON)) + (P(),) * 7,
        out_specs=(cells, cells, P(), P(), P(), P()),
        check_vma=False,
    )
```
